32 devices in a mesh: seq: 8 (over z, x), head: 4 (over y, core).
Axes of the slice: x: 2, y: 2, z: 4, core: 2. Of those that a mesh axis runs over, the one named last changes fastest.
Arguments:
- hidden: bfloat16 [4096, 3584], P('seq'), may hold values from -6 to 6
- norm_gain: float32 [3584], replicated, may hold values from 0.1 to 1.9
- query_weight: bfloat16 [3584, 3584], P('seq', 'head'), may hold values from -0.09375 to 0.09375
- query_bias: float32 [3584], P('head'), may hold values from -8 to 8
- keyval_weight: bfloat16 [3584, 2, 512], P('seq', None, 'head'), may hold values from -0.09375 to 0.09375
- keyval_bias: float32 [2, 512], P(None, 'head'), may hold values from -8 to 8
- beacon_weight: bfloat16 [3584, 2, 512], P('seq', None, 'head'), may hold values from -0.375 to 0.375
- beacon_bias: float32 [2, 512], P(None, 'head'), may hold values from -8 to 8
- out_weight: bfloat16 [3584, 3584], P('head', 'seq'), may hold values from -0.09375 to 0.09375
- ratios: int32 [2], replicated, may hold values from 8 to 32, as said below
Outputs:
- layer_out: bfloat16 [4096, 3584], P('seq', 'head')
The draws below stay inside these ranges and needn't reach their ends.
Inputs may be any that keep to these rules, and one draw needn't show every extreme that they name: `ratios`: each ratio is a whole number; at least one segment has ratio 8 and at least one has ratio 4 * 8.
All inputs are finite; a program needn't handle non-finite values.
Results may differ from the reference program's by a relative error of at most 0.012.
The reference program's roundings to bfloat16 on the way count: a program that leaves them out, or rounds other values in their place, can miss the bound.
Values may be sent and summed in bfloat16 or wider, within the bound.
No kernel may reach another device: no remote copies, remote signals or barrier semaphores. Data moves between devices by JAX's collectives and lax.ppermute only.
A program may use at most 192 MiB of HBM per device.

```python
import math
import jax
import jax.numpy as jnp
from jax import lax

D = 3584
QH = 28
KVH = 4
HEAD_DIM = 128
SEG = 2048
SPLIT = 4
R_MIN = 8
TOK_DEV = 512
TOKENS = 4096
NSEGS = 2
NB = 64
SLOTS = 512
QW = 3584
KW = 512
QW_DEV = 896
N_SEQ = 8
N_HEAD = 4


def draw_query_bias(key, part):
    values = 0.5 * jax.random.normal(jax.random.fold_in(key, 923), (QH, HEAD_DIM), jnp.float32)
    return jnp.clip(values, -8.0, 8.0).reshape(QH * HEAD_DIM)


def biased_pair(key, salt):
    value_part = 0.5 * jax.random.normal(jax.random.fold_in(key, salt), (KVH, HEAD_DIM), jnp.float32)
    key_part = 0.5 * jax.random.normal(jax.random.fold_in(key, salt + 2), (KVH, HEAD_DIM), jnp.float32)
    stacked = jnp.stack([key_part.reshape(KVH * HEAD_DIM), value_part.reshape(KVH * HEAD_DIM)], axis=0)
    return jnp.clip(stacked, -8.0, 8.0)


def draw_keyval_bias(key, part):
    return biased_pair(key, 941)


def draw_beacon_bias(key, part):
    return biased_pair(key, 951)


def draw_ratios(key, part):
    key = jax.random.fold_in(key, 937)
    values = jax.random.randint(jax.random.fold_in(key, 1), (NSEGS,), R_MIN, 4 * R_MIN + 1)
    smallest = jax.random.randint(jax.random.fold_in(key, 2), (), 0, NSEGS)
    step_away = jax.random.randint(jax.random.fold_in(key, 3), (), 1, NSEGS)
    largest = (smallest + step_away) % NSEGS
    positions = jnp.arange(NSEGS, dtype=jnp.int32)
    values = jnp.where(positions == largest, 4 * R_MIN, values)
    return jnp.where(positions == smallest, R_MIN, values).astype(jnp.int32)


def shard_levels(stream_key, extent, cuts, low, high):
    gain = 1.0
    for position, blocks in cuts:
        steps = jax.random.uniform(jax.random.fold_in(jax.random.fold_in(stream_key, 6), position), (blocks,), jnp.float32, low / len(cuts), high / len(cuts))
        gain = gain * jnp.repeat(jnp.exp(steps), extent[position] // blocks).reshape((-1,) + (1,) * (len(extent) - 1 - position))
    return gain


def scatter_about(key, extent, deviation, bound, cuts=(), kind=jnp.bfloat16):
    level = shard_levels(key, extent, cuts, -0.22, 0.18) if cuts else 1.0
    result = jax.random.normal(key, extent, jnp.float32) * deviation * level
    return jnp.minimum(jnp.maximum(result, -bound), bound).astype(kind)


def setup_inputs(seed: int = 0) -> dict:
    streams_of = jax.random.split(jax.random.key(seed), 11)
    hidden = scatter_about(streams_of[0], (TOKENS, D), 1.0, 6.0, ((0, 8),))
    norm_gain = jnp.clip(1.0 + 0.18 * jax.random.normal(streams_of[1], (D,), jnp.float32), 0.1, 1.9)
    query_weight = scatter_about(streams_of[2], (D, QW), D ** -0.5, 0.09375, ((0, 8), (1, 4)))
    query_bias = draw_query_bias(jax.random.fold_in(streams_of[10], 71), 0)
    keyval_weight = scatter_about(streams_of[4], (D, 2, KW), D ** -0.5, 0.09375, ((0, 8), (2, 4)))
    keyval_bias = draw_keyval_bias(jax.random.fold_in(streams_of[10], 71), 0)
    beacon_weight = scatter_about(streams_of[6], (D, 2, KW), (D // 16) ** -0.5, 0.375, ((0, 8), (2, 4)))
    beacon_bias = draw_beacon_bias(jax.random.fold_in(streams_of[10], 71), 0)
    out_weight = scatter_about(streams_of[8], (QW, D), QW ** -0.5, 0.09375, ((0, 4), (1, 8)))
    ratios = draw_ratios(jax.random.fold_in(streams_of[10], 71), 0)
    return {"hidden": hidden, "norm_gain": norm_gain, "query_weight": query_weight, "query_bias": query_bias, "keyval_weight": keyval_weight, "keyval_bias": keyval_bias, "beacon_weight": beacon_weight, "beacon_bias": beacon_bias, "out_weight": out_weight, "ratios": ratios}


def reference(hidden, norm_gain, query_weight, query_bias, keyval_weight, keyval_bias, beacon_weight, beacon_bias, out_weight, ratios):
    floats = hidden.astype(jnp.float32)
    normed = (floats * lax.rsqrt(lax.optimization_barrier(jnp.mean(floats * floats, axis=1, keepdims=True)) + 1e-06) * norm_gain).astype(jnp.bfloat16)
    query = (jnp.dot(normed, query_weight, preferred_element_type=jnp.float32) + query_bias).astype(jnp.bfloat16)
    keyval = (jnp.dot(normed, keyval_weight.reshape(D, 2 * KW), preferred_element_type=jnp.float32).reshape(TOKENS, 2, KW) + keyval_bias).astype(jnp.bfloat16)
    block_ratio = jnp.repeat(ratios, SPLIT)
    slot_ids = jnp.arange(NB, dtype=jnp.int32)
    token_ids = jnp.arange(TOK_DEV, dtype=jnp.int32)
    member = (token_ids[None, None, :] // block_ratio[:, None, None] == slot_ids[None, :, None]) & (slot_ids[None, :, None] < TOK_DEV // block_ratio[:, None, None])
    pooled_sum = jnp.einsum('bgi,bid->bgd', member.astype(jnp.float32), normed.reshape(N_SEQ, TOK_DEV, D).astype(jnp.float32))
    pooled = (pooled_sum / block_ratio[:, None, None].astype(jnp.float32)).astype(jnp.bfloat16).reshape(SLOTS, D)
    beacon = (jnp.dot(pooled, beacon_weight.reshape(D, 2 * KW), preferred_element_type=jnp.float32).reshape(SLOTS, 2, KW) + beacon_bias).astype(jnp.bfloat16)
    slot_live = (slot_ids[None, :] < TOK_DEV // block_ratio[:, None]).reshape(SLOTS)
    slot_segment = jnp.arange(SLOTS, dtype=jnp.int32) // NB // SPLIT
    groups = QH // KVH

    def attend(block_index):
        segment = block_index // SPLIT
        seg_place = block_index % SPLIT
        queries = lax.dynamic_slice_in_dim(query, block_index * TOK_DEV, TOK_DEV, 0).reshape(TOK_DEV, KVH, groups, HEAD_DIM).astype(jnp.float32)
        segment_kv = lax.dynamic_slice_in_dim(keyval, segment * SEG, SEG, 0)
        all_keys = jnp.concatenate([segment_kv, beacon], axis=0).astype(jnp.float32)
        key_pos = jnp.arange(SEG, dtype=jnp.int32)
        query_pos = seg_place * TOK_DEV + token_ids
        raw_mask = key_pos[None, :] <= query_pos[:, None]
        beacon_mask = jnp.broadcast_to((slot_live & (slot_segment < segment))[None, :], (TOK_DEV, SLOTS))
        full_mask = jnp.concatenate([raw_mask, beacon_mask], axis=1)
        key_heads = all_keys[:, 0].reshape(SEG + SLOTS, KVH, HEAD_DIM)
        value_heads = all_keys[:, 1].reshape(SEG + SLOTS, KVH, HEAD_DIM)
        scores = jnp.einsum('tkgd,ukd->kgtu', queries, key_heads) / math.sqrt(HEAD_DIM)
        scores = jnp.where(full_mask[None, None], scores, -1e+30)
        row_max = lax.optimization_barrier(jnp.max(scores, axis=3, keepdims=True))
        weights = jnp.exp(scores - row_max)
        denominator = lax.optimization_barrier(jnp.sum(weights, axis=3))
        rounded = lax.optimization_barrier(weights.astype(jnp.bfloat16)).astype(jnp.float32)
        weighted = jnp.einsum('kgtu,ukd->tkgd', rounded, value_heads) / jnp.transpose(denominator, (2, 0, 1))[..., None]
        return weighted.reshape(TOK_DEV, QW).astype(jnp.bfloat16)
    attention = lax.map(attend, jnp.arange(N_SEQ, dtype=jnp.int32)).reshape(TOKENS, QW)
    total_out = jnp.zeros((TOKENS, D), jnp.float32)
    for head_group in range(N_HEAD):
        columns = attention[:, head_group * QW_DEV:(head_group + 1) * QW_DEV]
        partial_value = jnp.dot(columns, out_weight[head_group * QW_DEV:(head_group + 1) * QW_DEV], preferred_element_type=jnp.float32)
        total_out = total_out + lax.optimization_barrier(partial_value.astype(jnp.bfloat16)).astype(jnp.float32)
    return total_out.astype(jnp.bfloat16)
```

```python
import functools
import math

import jax
import jax.numpy as jnp
from jax import lax
from jax.experimental import pallas as pl
from jax.experimental.pallas import tpu as pltpu
from jax.sharding import PartitionSpec as P

QH = 28
KVH = 4
HEAD_DIM = 128
SPLIT = 4
R_MIN = 8
AXES = ("seq", "head")
VMEM_LIMIT = 56 * 1024 * 1024


def params():
    return pltpu.CompilerParams(vmem_limit_bytes=VMEM_LIMIT)


def vmem():
    return pl.BlockSpec(memory_space=pltpu.VMEM)


def smem():
    return pl.BlockSpec(memory_space=pltpu.SMEM)


def hbm():
    return pl.BlockSpec(memory_space=pl.ANY)


def moves(n_seq, rule):
    pairs = []
    for s in range(n_seq):
        for h in range(KVH):
            target = rule(s >> 2, (s >> 1) & 1, s & 1, h >> 1, h & 1)
            if target is not None:
                big, l, x, y, c = target
                pairs.append((s * KVH + h, (4 * big + 2 * l + x) * KVH + 2 * y + c))
    return pairs


def send(value, n_seq, rule):
    return lax.ppermute(value, AXES, moves(n_seq, rule))


def norm_kernel(info, hidden, first, second, gain, normed, pooled, buf, sems):
    rows = hidden.shape[0]
    half = rows // 2
    tiles = sems.shape[0]
    tile = rows // tiles
    matched, y_bit, ratio = info[0], info[1], info[2]

    def land(i):
        return buf.at[pl.ds(i * tile, tile), :]

    for i in range(tiles):

        @pl.when(matched == 1)
        def _():
            pltpu.make_async_copy(hidden.at[pl.ds(i * tile, tile), :], land(i), sems.at[i]).start()

        upper = (i * tile) // half
        local = pl.ds(i * tile - upper * half, tile)

        @pl.when((matched == 0) & (y_bit == upper))
        def _():
            pltpu.make_async_copy(first.at[local, :], land(i), sems.at[i]).start()

        @pl.when((matched == 0) & (y_bit != upper))
        def _():
            pltpu.make_async_copy(second.at[local, :], land(i), sems.at[i]).start()

    scale = gain[...]
    for i in range(tiles):
        pltpu.make_async_copy(hidden.at[pl.ds(i * tile, tile), :], land(i), sems.at[i]).wait()
        floats = buf[i * tile : (i + 1) * tile, :].astype(jnp.float32)
        mean = jnp.mean(floats * floats, axis=1, keepdims=True)
        normed[i * tile : (i + 1) * tile, :] = (floats * lax.rsqrt(mean + 1e-06) * scale).astype(
            jnp.bfloat16
        )
    slots = pooled.shape[0]
    token = lax.broadcasted_iota(jnp.int32, (slots, rows), 1)
    slot = lax.broadcasted_iota(jnp.int32, (slots, rows), 0)
    member = (
        (token >= slot * ratio) & (token < (slot + 1) * ratio) & (slot < info[3])
    ).astype(jnp.float32).astype(jnp.bfloat16)
    total = jnp.dot(member, normed[...], preferred_element_type=jnp.float32)
    pooled[...] = (total / ratio.astype(jnp.float32)).astype(jnp.bfloat16)


def norm_and_pool(info, hidden, first, second, gain):
    rows, width = hidden.shape
    tiles = 8
    return pl.pallas_call(
        norm_kernel,
        out_shape=(
            jax.ShapeDtypeStruct((rows, width), jnp.bfloat16),
            jax.ShapeDtypeStruct((rows // R_MIN, width), jnp.bfloat16),
        ),
        in_specs=[smem(), hbm(), hbm(), hbm(), vmem()],
        out_specs=(vmem(), vmem()),
        scratch_shapes=[pltpu.VMEM((rows, width), jnp.bfloat16), pltpu.SemaphoreType.DMA((tiles,))],
        compiler_params=params(),
        cost_estimate=pl.CostEstimate(
            flops=2 * rows * rows // R_MIN * width, bytes_accessed=4 * rows * width, transcendentals=0
        ),
        name="norm_pool",
    )(info, hidden, first, second, gain.reshape(1, width))


def fetch_weights(info, refs, weights, sems, count):
    matched, big, l, x = info[0], info[4], info[5], info[6]
    rows = refs[0].shape[0] // 2
    own, copied = refs[:count], refs[count:]
    half = count // 2

    def spot(i, j):
        flip, m = i // half, i % half
        block = 4 * (big ^ m) + 2 * (l ^ j) + (x ^ flip)
        return weights.at[pl.ds(pl.multiple_of(block * rows, 16), rows), :]

    for i in range(count):
        for j in range(2):
            part = pl.ds(j * rows, rows)

            @pl.when(matched == 1)
            def _():
                pltpu.make_async_copy(own[i].at[part, :], spot(i, j), sems.at[2 * i + j]).start()

            @pl.when(matched == 0)
            def _():
                pltpu.make_async_copy(copied[i].at[part, :], spot(i, j), sems.at[2 * i + j]).start()

    for i in range(count):
        for j in range(2):
            pltpu.make_async_copy(
                own[i].at[pl.ds(j * rows, rows), :], spot(i, j), sems.at[2 * i + j]
            ).wait()


def query_kernel(count, info, normed, bias, *rest):
    refs, (out, weights, sems) = rest[: 2 * count], rest[2 * count :]
    fetch_weights(info, refs, weights, sems, count)
    tile = 256
    for i in range(out.shape[0] // tile):
        rows = slice(i * tile, (i + 1) * tile)
        product = jnp.dot(normed[rows, :], weights[...], preferred_element_type=jnp.float32)
        out[rows, :] = (product + bias[...]).astype(jnp.bfloat16)


def keyval_kernel(count, info, normed, pooled, bias, *rest):
    refs, (out, weights, sems) = rest[: 2 * count], rest[2 * count :]
    fetch_weights(info, refs, weights, sems, count)
    rows = normed.shape[0]
    cols = out.shape[1]
    product = jnp.dot(normed[...], weights[:, :cols], preferred_element_type=jnp.float32)
    out[:rows, :] = (product + bias[:, :cols]).astype(jnp.bfloat16)
    product = jnp.dot(pooled[...], weights[:, cols:], preferred_element_type=jnp.float32)
    out[rows:, :] = (product + bias[:, cols:]).astype(jnp.bfloat16)


def project(kernel, out_rows, out_cols, info, left, bias, own, copied):
    count = len(own)
    width = left[0].shape[1]
    cols = own[0].shape[1]
    return pl.pallas_call(
        functools.partial(kernel, count),
        out_shape=jax.ShapeDtypeStruct((out_rows, out_cols), jnp.bfloat16),
        in_specs=[smem()] + [vmem()] * (len(left) + 1) + [hbm()] * (2 * count),
        out_specs=vmem(),
        scratch_shapes=[
            pltpu.VMEM((width, cols), jnp.bfloat16),
            pltpu.SemaphoreType.DMA((2 * count,)),
        ],
        compiler_params=params(),
        cost_estimate=pl.CostEstimate(
            flops=2 * out_rows * out_cols * width,
            bytes_accessed=2 * width * (out_rows + cols),
            transcendentals=0,
        ),
        name="project",
    )(info, *left, bias.reshape(1, -1), *own, *copied)


def attend_kernel(tokens, beacons, info, ratios, queries, pair, far_pair, *rest):
    beacon_refs, out = rest[:beacons], rest[beacons]
    place = 2 * info[7] + info[6]
    big = info[4]
    scale = 1.0 / math.sqrt(HEAD_DIM)
    stride = pair.shape[0] // 2
    slots = stride - tokens
    tile = min(256, tokens)

    def pieces(variant):
        full = []
        if variant in (1, 3):
            full.append((pair, stride))
        if variant in (2, 3):
            full += [(far_pair, 0), (far_pair, stride)]
        return full

    def score(rows, keys):
        return lax.dot_general(
            rows, keys, (((1,), (1,)), ((), ())), preferred_element_type=jnp.float32
        ) * scale

    def run(variant):
        for start in range(0, tokens, tile):
            rows = queries[start : start + tile, :]
            parts = []
            seen = start + tile
            scores = score(rows, pair[:seen, :HEAD_DIM])
            q_pos = start + lax.broadcasted_iota(jnp.int32, (tile, seen), 0)
            k_pos = lax.broadcasted_iota(jnp.int32, (tile, seen), 1)
            parts.append((jnp.where(k_pos <= q_pos, scores, -1e30), pair[:seen, HEAD_DIM:]))
            for ref, offset in pieces(variant):
                parts.append(
                    (
                        score(rows, ref[offset : offset + tokens, :HEAD_DIM]),
                        ref[offset : offset + tokens, HEAD_DIM:],
                    )
                )
            for m in range(beacons):
                source = big ^ (m + 1)
                count = beacon_refs[m].shape[0]
                live = jnp.where(source < big, tokens // ratios[source], 0)
                local = lax.broadcasted_iota(jnp.int32, (tile, count), 1) % slots
                scores = score(rows, beacon_refs[m][:, :HEAD_DIM])
                parts.append((jnp.where(local < live, scores, -1e30), beacon_refs[m][:, HEAD_DIM:]))
            top = functools.reduce(
                jnp.maximum, [jnp.max(s, axis=1, keepdims=True) for s, _ in parts]
            )
            total = jnp.zeros((tile, 1), jnp.float32)
            mixed = jnp.zeros((tile, HEAD_DIM), jnp.float32)
            for scores, values in parts:
                weights = jnp.exp(scores - top)
                total += jnp.sum(weights, axis=1, keepdims=True)
                mixed += jnp.dot(
                    weights.astype(jnp.bfloat16), values, preferred_element_type=jnp.float32
                )
            out[start : start + tile, :] = (mixed / total).astype(jnp.bfloat16)

    for variant in range(SPLIT):
        pl.when(place == variant)(functools.partial(run, variant))


def attend(info, ratios, queries, pair, far_pair, beacons):
    tokens, cols = queries.shape
    heads = cols // HEAD_DIM
    keys = 4 * tokens + sum(b.shape[0] for b in beacons)
    return pl.pallas_call(
        functools.partial(attend_kernel, tokens, len(beacons)),
        grid=(heads,),
        out_shape=jax.ShapeDtypeStruct((tokens, cols), jnp.bfloat16),
        in_specs=[
            smem(),
            smem(),
            pl.BlockSpec((tokens, HEAD_DIM), lambda i: (0, i)),
            vmem(),
            vmem(),
        ]
        + [vmem()] * len(beacons),
        out_specs=pl.BlockSpec((tokens, HEAD_DIM), lambda i: (0, i)),
        compiler_params=params(),
        cost_estimate=pl.CostEstimate(
            flops=4 * tokens * keys * cols,
            bytes_accessed=4 * tokens * cols,
            transcendentals=tokens * keys * heads,
        ),
        name="attend",
    )(info, ratios, queries, pair, far_pair, *beacons)


def out_kernel(core_flip, info, attention, weights, out):
    width = out.shape[2]
    for j in range(2):
        group = 2 * (info[1] ^ j) + (info[7] ^ core_flip)
        block = weights[pl.ds(pl.multiple_of(group * width, 16), width), :]
        out[j] = lax.dot_general(
            attention[...], block, (((1,), (1,)), ((), ())), preferred_element_type=jnp.float32
        ).astype(jnp.bfloat16)


def out_project(core_flip, info, attention, weights):
    tokens, depth = attention.shape
    width = weights.shape[0] // KVH
    return pl.pallas_call(
        functools.partial(out_kernel, core_flip),
        out_shape=jax.ShapeDtypeStruct((2, tokens, width), jnp.bfloat16),
        in_specs=[smem(), vmem(), vmem()],
        out_specs=vmem(),
        compiler_params=params(),
        cost_estimate=pl.CostEstimate(
            flops=4 * tokens * width * depth, bytes_accessed=4 * width * depth, transcendentals=0
        ),
        name="out_project",
    )(info, attention, weights)


def gather_pieces(shard, n_seq):
    other = send(
        shard, n_seq, lambda big, l, x, y, c: (big, 1 - l, x, y, c) if c != l else None
    )
    near = [jnp.concatenate([shard, other], axis=0)]
    bit = 1
    while bit < n_seq // SPLIT:
        near += [
            send(
                piece,
                n_seq,
                lambda big, l, x, y, c: (big ^ bit, l, x, y, c) if c == l else None,
            )
            for piece in near
        ]
        bit *= 2
    across = [
        send(piece, n_seq, lambda big, l, x, y, c: (big, l, 1 - x, y, c) if c == l else None)
        for piece in near
    ]
    own = near + across
    copied = [
        send(piece, n_seq, lambda big, l, x, y, c: (big, l, x, y, 1 - c) if c == l else None)
        for piece in own
    ]
    return own, copied


def on_device(
    hidden,
    norm_gain,
    query_weight,
    query_bias,
    keyval_weight,
    keyval_bias,
    beacon_weight,
    beacon_bias,
    out_weight,
    ratios,
):
    n_seq = lax.axis_size("seq")
    rows_dev = hidden.shape[0]
    half = rows_dev // 2
    seq_index = lax.axis_index("seq")
    head_index = lax.axis_index("head")
    big, l, x = seq_index // 4, (seq_index // 2) % 2, seq_index % 2
    y, c = head_index // 2, head_index % 2
    matched = c == l
    segment_ids = jnp.arange(ratios.shape[0], dtype=jnp.int32)
    own_ratio = jnp.sum(jnp.where(segment_ids == big, ratios, 0))
    info = jnp.stack(
        [matched.astype(jnp.int32), y, own_ratio, rows_dev // own_ratio, big, l, x, c]
    ).astype(jnp.int32)

    own_half = lax.dynamic_slice_in_dim(hidden, y * half, half, 0)
    first = send(
        own_half, n_seq, lambda big, l, x, y, c: (big, 1 - l, x, y, 1 - c) if c != l else None
    )
    second = send(first, n_seq, lambda big, l, x, y, c: (big, l, x, 1 - y, c) if c != l else None)

    kv_cols = 2 * keyval_weight.shape[2]
    depth = keyval_weight.shape[0]
    small = jnp.concatenate(
        [keyval_weight.reshape(depth, kv_cols), beacon_weight.reshape(depth, kv_cols)], axis=1
    )
    biases = jnp.concatenate([query_bias, keyval_bias.reshape(-1), beacon_bias.reshape(-1)])
    other_biases = send(biases, n_seq, lambda big, l, x, y, c: (big, l, x, y, 1 - c))
    biases = jnp.where(matched, biases, other_biases)
    query_cols = query_weight.shape[1]

    small_own, small_copied = gather_pieces(small, n_seq)
    query_own, query_copied = gather_pieces(query_weight, n_seq)
    out_rows = lax.all_gather(out_weight.T, "seq", axis=0, tiled=True)

    normed, pooled = norm_and_pool(info, hidden, first, second, norm_gain)
    slots_dev = rows_dev // R_MIN
    keyval = project(
        keyval_kernel,
        rows_dev + slots_dev,
        kv_cols,
        info,
        [normed, pooled],
        biases[query_cols:],
        small_own,
        small_copied,
    )
    beside = send(keyval, n_seq, lambda big, l, x, y, c: (big, l, 1 - x, y, c))
    pair = jnp.concatenate([keyval, beside], axis=0)
    far_pair = send(pair, n_seq, lambda big, l, x, y, c: (big, l, x, y, 1 - c))
    stride = rows_dev + slots_dev
    beacons = [
        jnp.concatenate(
            [
                pair[rows_dev:stride],
                pair[stride + rows_dev :],
                far_pair[rows_dev:stride],
                far_pair[stride + rows_dev :],
            ],
            axis=0,
        )
    ]
    bit = 1
    while bit < n_seq // SPLIT:
        beacons += [
            send(piece, n_seq, lambda big, l, x, y, c: (big ^ bit, l, x, y, c)) for piece in beacons
        ]
        bit *= 2
    query = project(
        query_kernel,
        rows_dev,
        query_cols,
        info,
        [normed],
        biases[:query_cols],
        query_own,
        query_copied,
    )
    attention = attend(info, ratios, query, pair, far_pair, beacons[1:])
    swapped = send(
        attention, n_seq, lambda big, l, x, y, c: (big, 1 - l, x, y, 1 - c) if c != l else None
    )
    attention = jnp.where(matched, attention, swapped)

    away = out_project(1, info, attention, out_rows)
    from_core = send(away, n_seq, lambda big, l, x, y, c: (big, l, x, y, 1 - c))
    kept = out_project(0, info, attention, out_rows)
    sums = kept.astype(jnp.float32) + from_core.astype(jnp.float32)
    from_y = send(
        sums[1].astype(jnp.bfloat16), n_seq, lambda big, l, x, y, c: (big, l, x, 1 - y, c)
    )
    return (sums[0] + from_y.astype(jnp.float32)).astype(jnp.bfloat16)


def solution(mesh):
    return jax.shard_map(
        on_device,
        mesh=mesh,
        in_specs=(
            P("seq", None),
            P(),
            P("seq", "head"),
            P("head"),
            P("seq", None, "head"),
            P(None, "head"),
            P("seq", None, "head"),
            P(None, "head"),
            P("head", "seq"),
            P(),
        ),
        out_specs=P("seq", "head"),
        check_vma=False,
    )
```

```python
import functools
import math

import jax
import jax.numpy as jnp
from jax import lax
from jax.experimental import pallas as pl
from jax.experimental.pallas import tpu as pltpu
from jax.sharding import PartitionSpec as P

QH = 28
KVH = 4
HEAD_DIM = 128
SPLIT = 4
R_MIN = 8
AXES = ("seq", "head")
VMEM_LIMIT = 56 * 1024 * 1024


def params():
    return pltpu.CompilerParams(vmem_limit_bytes=VMEM_LIMIT)


def vmem():
    return pl.BlockSpec(memory_space=pltpu.VMEM)


def smem():
    return pl.BlockSpec(memory_space=pltpu.SMEM)


def hbm():
    return pl.BlockSpec(memory_space=pl.ANY)


def moves(n_seq, rule):
    pairs = []
    for s in range(n_seq):
        for h in range(KVH):
            target = rule(s >> 2, (s >> 1) & 1, s & 1, h >> 1, h & 1)
            if target is not None:
                big, l, x, y, c = target
                pairs.append((s * KVH + h, (4 * big + 2 * l + x) * KVH + 2 * y + c))
    return pairs


def send(value, n_seq, rule):
    return lax.ppermute(value, AXES, moves(n_seq, rule))


def norm_kernel(info, hidden, first, second, gain, normed, pooled, buf, sems):
    rows = hidden.shape[0]
    half = rows // 2
    tiles = sems.shape[0]
    tile = rows // tiles
    matched, y_bit, ratio = info[0], info[1], info[2]

    def land(i):
        return buf.at[pl.ds(i * tile, tile), :]

    for i in range(tiles):

        @pl.when(matched == 1)
        def _():
            pltpu.make_async_copy(hidden.at[pl.ds(i * tile, tile), :], land(i), sems.at[i]).start()

        upper = (i * tile) // half
        local = pl.ds(i * tile - upper * half, tile)

        @pl.when((matched == 0) & (y_bit == upper))
        def _():
            pltpu.make_async_copy(first.at[local, :], land(i), sems.at[i]).start()

        @pl.when((matched == 0) & (y_bit != upper))
        def _():
            pltpu.make_async_copy(second.at[local, :], land(i), sems.at[i]).start()

    scale = gain[...]
    for i in range(tiles):
        pltpu.make_async_copy(hidden.at[pl.ds(i * tile, tile), :], land(i), sems.at[i]).wait()
        floats = buf[i * tile : (i + 1) * tile, :].astype(jnp.float32)
        mean = jnp.mean(floats * floats, axis=1, keepdims=True)
        normed[i * tile : (i + 1) * tile, :] = (floats * lax.rsqrt(mean + 1e-06) * scale).astype(
            jnp.bfloat16
        )
    slots = pooled.shape[0]
    token = lax.broadcasted_iota(jnp.int32, (slots, rows), 1)
    slot = lax.broadcasted_iota(jnp.int32, (slots, rows), 0)
    member = (
        (token >= slot * ratio) & (token < (slot + 1) * ratio) & (slot < info[3])
    ).astype(jnp.float32).astype(jnp.bfloat16)
    total = jnp.dot(member, normed[...], preferred_element_type=jnp.float32)
    pooled[...] = (total / ratio.astype(jnp.float32)).astype(jnp.bfloat16)


def norm_and_pool(info, hidden, first, second, gain):
    rows, width = hidden.shape
    tiles = 8
    return pl.pallas_call(
        norm_kernel,
        out_shape=(
            jax.ShapeDtypeStruct((rows, width), jnp.bfloat16),
            jax.ShapeDtypeStruct((rows // R_MIN, width), jnp.bfloat16),
        ),
        in_specs=[smem(), hbm(), hbm(), hbm(), vmem()],
        out_specs=(vmem(), vmem()),
        scratch_shapes=[pltpu.VMEM((rows, width), jnp.bfloat16), pltpu.SemaphoreType.DMA((tiles,))],
        compiler_params=params(),
        cost_estimate=pl.CostEstimate(
            flops=2 * rows * rows // R_MIN * width, bytes_accessed=4 * rows * width, transcendentals=0
        ),
        name="norm_pool",
    )(info, hidden, first, second, gain.reshape(1, width))


def fetch_weights(info, refs, weights, sems, count):
    matched, big, l, x, swap = info[0], info[4], info[5], info[6], info[8]
    rows = refs[0].shape[0] // 2
    own, copied = refs[:count], refs[count:]
    half = count // 2

    def copy(source, i, j):
        flip, m = i // half, i % half
        place = j if (copied or m == 0) else j ^ swap
        block = 4 * (big ^ m) + 2 * (l ^ place) + (x ^ flip)
        return pltpu.make_async_copy(
            source[i].at[pl.ds(j * rows, rows), :],
            weights.at[pl.ds(pl.multiple_of(block * rows, 16), rows), :],
            sems.at[2 * i + j],
        )

    for i in range(count):
        for j in range(2):
            if copied:
                pl.when(matched == 1)(copy(own, i, j).start)
                pl.when(matched == 0)(copy(copied, i, j).start)
            else:
                copy(own, i, j).start()
    for i in range(count):
        for j in range(2):
            copy(own, i, j).wait()


def query_kernel(count, info, normed, bias, *rest):
    refs, (out, weights, sems) = rest[: 2 * count], rest[2 * count :]
    fetch_weights(info, refs, weights, sems, count)
    tile = 256
    for i in range(out.shape[0] // tile):
        rows = slice(i * tile, (i + 1) * tile)
        product = jnp.dot(normed[rows, :], weights[...], preferred_element_type=jnp.float32)
        out[rows, :] = (product + bias[...]).astype(jnp.bfloat16)


def keyval_kernel(count, info, normed, pooled, bias, *rest):
    refs, (out, weights, sems) = rest[: 2 * count], rest[2 * count :]
    fetch_weights(info, refs, weights, sems, count)
    rows = normed.shape[0]
    cols = out.shape[1]
    product = jnp.dot(normed[...], weights[:, :cols], preferred_element_type=jnp.float32)
    out[:rows, :] = (product + bias[:, :cols]).astype(jnp.bfloat16)
    product = jnp.dot(pooled[...], weights[:, cols:], preferred_element_type=jnp.float32)
    out[rows:, :] = (product + bias[:, cols:]).astype(jnp.bfloat16)


def project(kernel, out_rows, out_cols, info, left, bias, own, copied):
    count = len(own)
    width = left[0].shape[1]
    cols = own[0].shape[1]
    return pl.pallas_call(
        functools.partial(kernel, count),
        out_shape=jax.ShapeDtypeStruct((out_rows, out_cols), jnp.bfloat16),
        in_specs=[smem()] + [vmem()] * (len(left) + 1) + [hbm()] * (2 * count),
        out_specs=vmem(),
        scratch_shapes=[
            pltpu.VMEM((width, cols), jnp.bfloat16),
            pltpu.SemaphoreType.DMA((2 * count,)),
        ],
        compiler_params=params(),
        cost_estimate=pl.CostEstimate(
            flops=2 * out_rows * out_cols * width,
            bytes_accessed=2 * width * (out_rows + cols),
            transcendentals=0,
        ),
        name="project",
    )(info, *left, bias.reshape(1, -1), *own, *copied)


def attend_kernel(tokens, beacons, first_row, info, ratios, queries, pair, far_pair, *rest):
    beacon_refs, out = rest[:beacons], rest[beacons]
    place = 2 * info[7] + info[6]
    big = info[4]
    scale = 1.0 / math.sqrt(HEAD_DIM)
    stride = pair.shape[0] // 2
    slots = stride - tokens
    tile = min(256, tokens)

    def pieces(variant):
        full = []
        if variant in (1, 3):
            full.append((pair, stride))
        if variant in (2, 3):
            full += [(far_pair, 0), (far_pair, stride)]
        return full

    def score(rows, keys):
        return lax.dot_general(
            rows, keys, (((1,), (1,)), ((), ())), preferred_element_type=jnp.float32
        ) * scale

    def run(variant):
        for local_start in range(0, out.shape[0], tile):
            start = first_row + local_start
            rows = queries[start : start + tile, :]
            parts = []
            seen = start + tile
            scores = score(rows, pair[:seen, :HEAD_DIM])
            q_pos = start + lax.broadcasted_iota(jnp.int32, (tile, seen), 0)
            k_pos = lax.broadcasted_iota(jnp.int32, (tile, seen), 1)
            parts.append((jnp.where(k_pos <= q_pos, scores, -1e30), pair[:seen, HEAD_DIM:]))
            for ref, offset in pieces(variant):
                parts.append(
                    (
                        score(rows, ref[offset : offset + tokens, :HEAD_DIM]),
                        ref[offset : offset + tokens, HEAD_DIM:],
                    )
                )
            for m in range(beacons):
                source = big ^ (m + 1)
                count = beacon_refs[m].shape[0]
                live = jnp.where(source < big, tokens // ratios[source], 0)
                local = lax.broadcasted_iota(jnp.int32, (tile, count), 1) % slots
                scores = score(rows, beacon_refs[m][:, :HEAD_DIM])
                parts.append((jnp.where(local < live, scores, -1e30), beacon_refs[m][:, HEAD_DIM:]))
            top = functools.reduce(
                jnp.maximum, [jnp.max(s, axis=1, keepdims=True) for s, _ in parts]
            )
            total = jnp.zeros((tile, 1), jnp.float32)
            mixed = jnp.zeros((tile, HEAD_DIM), jnp.float32)
            for scores, values in parts:
                weights = jnp.exp(scores - top)
                total += jnp.sum(weights, axis=1, keepdims=True)
                mixed += jnp.dot(
                    weights.astype(jnp.bfloat16), values, preferred_element_type=jnp.float32
                )
            out[local_start : local_start + tile, :] = (mixed / total).astype(jnp.bfloat16)

    for variant in range(SPLIT):
        pl.when(place == variant)(functools.partial(run, variant))


def attend(first_row, row_count, info, ratios, queries, pair, far_pair, beacons):
    tokens, cols = queries.shape
    heads = cols // HEAD_DIM
    keys = 4 * tokens + sum(b.shape[0] for b in beacons)
    return pl.pallas_call(
        functools.partial(attend_kernel, tokens, len(beacons), first_row),
        grid=(heads,),
        out_shape=jax.ShapeDtypeStruct((row_count, cols), jnp.bfloat16),
        in_specs=[
            smem(),
            smem(),
            pl.BlockSpec((tokens, HEAD_DIM), lambda i: (0, i)),
            vmem(),
            vmem(),
        ]
        + [vmem()] * len(beacons),
        out_specs=pl.BlockSpec((row_count, HEAD_DIM), lambda i: (0, i)),
        compiler_params=params(),
        cost_estimate=pl.CostEstimate(
            flops=4 * row_count * keys * cols,
            bytes_accessed=4 * tokens * cols,
            transcendentals=row_count * keys * heads,
        ),
        name="attend",
    )(info, ratios, queries, pair, far_pair, *beacons)


def out_kernel(count, info, attention, *rest):
    refs, (out, weights, sems) = rest[:count], rest[count:]
    fetch_weights(info, refs, weights, sems, count)
    width = out.shape[3]
    for i in (1, 0):
        for j in (1, 0):
            group = 2 * (info[1] ^ j) + (info[7] ^ i)
            block = weights[pl.ds(pl.multiple_of(group * width, 16), width), :]
            out[i, j] = lax.dot_general(
                attention[...], block, (((1,), (1,)), ((), ())), preferred_element_type=jnp.float32
            ).astype(jnp.bfloat16)


def out_project(info, attention, pieces):
    tokens, depth = attention.shape
    count = len(pieces)
    width = count * pieces[0].shape[0] // KVH
    return pl.pallas_call(
        functools.partial(out_kernel, count),
        out_shape=jax.ShapeDtypeStruct((2, 2, tokens, width), jnp.bfloat16),
        in_specs=[smem(), vmem()] + [hbm()] * count,
        out_specs=vmem(),
        scratch_shapes=[
            pltpu.VMEM((KVH * width, depth), jnp.bfloat16),
            pltpu.SemaphoreType.DMA((2 * count,)),
        ],
        compiler_params=params(),
        cost_estimate=pl.CostEstimate(
            flops=8 * tokens * width * depth, bytes_accessed=8 * width * depth, transcendentals=0
        ),
        name="out_project",
    )(info, attention, *pieces)


def gather_pieces(shard, n_seq):
    other = send(
        shard, n_seq, lambda big, l, x, y, c: (big, 1 - l, x, y, c) if c != l else None
    )
    near = [jnp.concatenate([shard, other], axis=0)]
    bit = 1
    while bit < n_seq // SPLIT:
        near += [
            send(
                piece,
                n_seq,
                lambda big, l, x, y, c: (big ^ bit, l, x, y, c) if c == l else None,
            )
            for piece in near
        ]
        bit *= 2
    across = [
        send(piece, n_seq, lambda big, l, x, y, c: (big, l, 1 - x, y, c) if c == l else None)
        for piece in near
    ]
    own = near + across
    copied = [
        send(piece, n_seq, lambda big, l, x, y, c: (big, l, x, y, 1 - c) if c == l else None)
        for piece in own
    ]
    return own, copied


def gather_output_pieces(shard, inner, n_seq):
    other = send(shard, n_seq, lambda big, l, x, y, c: (big, 1 - l, x, y, c))
    near = [jnp.concatenate([shard, other], axis=0)]
    if n_seq == 2 * SPLIT:
        middle = send(
            near[0], n_seq, lambda big, l, x, y, c: (1 - big, 1 - l, x, y, c) if big != l else None
        )
        outer = send(
            middle, n_seq, lambda big, l, x, y, c: (big, 1 - l, x, y, c) if big != l else None
        )
        near.append(jnp.where(inner, middle, outer))
    else:
        bit = 1
        while bit < n_seq // SPLIT:
            near += [
                send(piece, n_seq, lambda big, l, x, y, c: (big ^ bit, l, x, y, c))
                for piece in near
            ]
            bit *= 2
    return near + [send(p, n_seq, lambda big, l, x, y, c: (big, l, 1 - x, y, c)) for p in near]


def on_device(
    hidden,
    norm_gain,
    query_weight,
    query_bias,
    keyval_weight,
    keyval_bias,
    beacon_weight,
    beacon_bias,
    out_weight,
    ratios,
):
    n_seq = lax.axis_size("seq")
    rows_dev = hidden.shape[0]
    half = rows_dev // 2
    seq_index = lax.axis_index("seq")
    head_index = lax.axis_index("head")
    big, l, x = seq_index // 4, (seq_index // 2) % 2, seq_index % 2
    y, c = head_index // 2, head_index % 2
    matched = c == l
    segment_ids = jnp.arange(ratios.shape[0], dtype=jnp.int32)
    own_ratio = jnp.sum(jnp.where(segment_ids == big, ratios, 0))
    inner = (big != l) & (n_seq == 2 * SPLIT)
    info = jnp.stack(
        [
            matched.astype(jnp.int32),
            y,
            own_ratio,
            rows_dev // own_ratio,
            big,
            l,
            x,
            c,
            inner.astype(jnp.int32),
        ]
    ).astype(jnp.int32)

    own_half = lax.dynamic_slice_in_dim(hidden, y * half, half, 0)
    first = send(
        own_half, n_seq, lambda big, l, x, y, c: (big, 1 - l, x, y, 1 - c) if c != l else None
    )
    second = send(first, n_seq, lambda big, l, x, y, c: (big, l, x, 1 - y, c) if c != l else None)

    kv_cols = 2 * keyval_weight.shape[2]
    depth = keyval_weight.shape[0]
    small = jnp.concatenate(
        [keyval_weight.reshape(depth, kv_cols), beacon_weight.reshape(depth, kv_cols)], axis=1
    )
    biases = jnp.concatenate([query_bias, keyval_bias.reshape(-1), beacon_bias.reshape(-1)])
    other_biases = send(biases, n_seq, lambda big, l, x, y, c: (big, l, x, y, 1 - c))
    biases = jnp.where(matched, biases, other_biases)
    query_cols = query_weight.shape[1]

    small_own, small_copied = gather_pieces(small, n_seq)
    query_own, query_copied = gather_pieces(query_weight, n_seq)
    out_shard, _ = lax.optimization_barrier((out_weight.T, query_own[1]))
    out_pieces = gather_output_pieces(out_shard, inner, n_seq)

    normed, pooled = norm_and_pool(info, hidden, first, second, norm_gain)
    slots_dev = rows_dev // R_MIN
    keyval = project(
        keyval_kernel,
        rows_dev + slots_dev,
        kv_cols,
        info,
        [normed, pooled],
        biases[query_cols:],
        small_own,
        small_copied,
    )
    beside = send(keyval, n_seq, lambda big, l, x, y, c: (big, l, 1 - x, y, c))
    pair = jnp.concatenate([keyval, beside], axis=0)
    far_pair = send(pair, n_seq, lambda big, l, x, y, c: (big, l, x, y, 1 - c))
    stride = rows_dev + slots_dev
    beacons = [
        jnp.concatenate(
            [
                pair[rows_dev:stride],
                pair[stride + rows_dev :],
                far_pair[rows_dev:stride],
                far_pair[stride + rows_dev :],
            ],
            axis=0,
        )
    ]
    bit = 1
    while bit < n_seq // SPLIT:
        beacons += [
            send(piece, n_seq, lambda big, l, x, y, c: (big ^ bit, l, x, y, c)) for piece in beacons
        ]
        bit *= 2
    query = project(
        query_kernel,
        rows_dev,
        query_cols,
        info,
        [normed],
        biases[:query_cols],
        query_own,
        query_copied,
    )
    parts = 2
    part = rows_dev // parts
    results = []
    for i in range(parts):
        attention = attend(i * part, part, info, ratios, query, pair, far_pair, beacons[1:])
        swapped = send(
            attention, n_seq, lambda big, l, x, y, c: (big, 1 - l, x, y, 1 - c) if c != l else None
        )
        attention = jnp.where(matched, attention, swapped)
        partial = out_project(info, attention, out_pieces)
        from_core = send(partial[1], n_seq, lambda big, l, x, y, c: (big, l, x, y, 1 - c))
        sums = partial[0].astype(jnp.float32) + from_core.astype(jnp.float32)
        from_y = send(
            sums[1].astype(jnp.bfloat16), n_seq, lambda big, l, x, y, c: (big, l, x, 1 - y, c)
        )
        results.append((sums[0] + from_y.astype(jnp.float32)).astype(jnp.bfloat16))
    return jnp.concatenate(results, axis=0)


def solution(mesh):
    return jax.shard_map(
        on_device,
        mesh=mesh,
        in_specs=(
            P("seq", None),
            P(),
            P("seq", "head"),
            P("head"),
            P("seq", None, "head"),
            P(None, "head"),
            P("seq", None, "head"),
            P(None, "head"),
            P("head", "seq"),
            P(),
        ),
        out_specs=P("seq", "head"),
        check_vma=False,
    )
```

```python
import functools
import math

import jax
import jax.numpy as jnp
from jax import lax
from jax.experimental import pallas as pl
from jax.experimental.pallas import tpu as pltpu
from jax.sharding import PartitionSpec as P

QH = 28
KVH = 4
HEAD_DIM = 128
SPLIT = 4
R_MIN = 8
AXES = ("seq", "head")
VMEM_LIMIT = 56 * 1024 * 1024


def params():
    return pltpu.CompilerParams(vmem_limit_bytes=VMEM_LIMIT)


def vmem():
    return pl.BlockSpec(memory_space=pltpu.VMEM)


def smem():
    return pl.BlockSpec(memory_space=pltpu.SMEM)


def hbm():
    return pl.BlockSpec(memory_space=pl.ANY)


def moves(n_seq, rule):
    pairs = []
    for s in range(n_seq):
        for h in range(KVH):
            target = rule(s >> 2, (s >> 1) & 1, s & 1, h >> 1, h & 1)
            if target is not None:
                big, l, x, y, c = target
                pairs.append((s * KVH + h, (4 * big + 2 * l + x) * KVH + 2 * y + c))
    return pairs


def send(value, n_seq, rule):
    return lax.ppermute(value, AXES, moves(n_seq, rule))


def norm_kernel(info, hidden, first, second, gain, normed, pooled, buf, sems):
    rows = hidden.shape[0]
    half = rows // 2
    tiles = sems.shape[0]
    tile = rows // tiles
    matched, y_bit, ratio = info[0], info[1], info[2]

    def land(i):
        return buf.at[pl.ds(i * tile, tile), :]

    for i in range(tiles):

        @pl.when(matched == 1)
        def _():
            pltpu.make_async_copy(hidden.at[pl.ds(i * tile, tile), :], land(i), sems.at[i]).start()

        upper = (i * tile) // half
        local = pl.ds(i * tile - upper * half, tile)

        @pl.when((matched == 0) & (y_bit == upper))
        def _():
            pltpu.make_async_copy(first.at[local, :], land(i), sems.at[i]).start()

        @pl.when((matched == 0) & (y_bit != upper))
        def _():
            pltpu.make_async_copy(second.at[local, :], land(i), sems.at[i]).start()

    scale = gain[...]
    for i in range(tiles):
        pltpu.make_async_copy(hidden.at[pl.ds(i * tile, tile), :], land(i), sems.at[i]).wait()
        floats = buf[i * tile : (i + 1) * tile, :].astype(jnp.float32)
        mean = jnp.mean(floats * floats, axis=1, keepdims=True)
        normed[i * tile : (i + 1) * tile, :] = (floats * lax.rsqrt(mean + 1e-06) * scale).astype(
            jnp.bfloat16
        )
    slots = pooled.shape[0]
    token = lax.broadcasted_iota(jnp.int32, (slots, rows), 1)
    slot = lax.broadcasted_iota(jnp.int32, (slots, rows), 0)
    member = (
        (token >= slot * ratio) & (token < (slot + 1) * ratio) & (slot < info[3])
    ).astype(jnp.float32).astype(jnp.bfloat16)
    total = jnp.dot(member, normed[...], preferred_element_type=jnp.float32)
    pooled[...] = (total / ratio.astype(jnp.float32)).astype(jnp.bfloat16)


def norm_and_pool(info, hidden, first, second, gain):
    rows, width = hidden.shape
    tiles = 8
    return pl.pallas_call(
        norm_kernel,
        out_shape=(
            jax.ShapeDtypeStruct((rows, width), jnp.bfloat16),
            jax.ShapeDtypeStruct((rows // R_MIN, width), jnp.bfloat16),
        ),
        in_specs=[smem(), hbm(), hbm(), hbm(), vmem()],
        out_specs=(vmem(), vmem()),
        scratch_shapes=[pltpu.VMEM((rows, width), jnp.bfloat16), pltpu.SemaphoreType.DMA((tiles,))],
        compiler_params=params(),
        cost_estimate=pl.CostEstimate(
            flops=2 * rows * rows // R_MIN * width, bytes_accessed=4 * rows * width, transcendentals=0
        ),
        name="norm_pool",
    )(info, hidden, first, second, gain.reshape(1, width))


def fetch_weights(info, keys, refs, weights, sems, first_col=0):
    matched, big, l, x = info[0], info[4], info[5], info[6]
    count = len(keys)
    rows, cols = refs[0].shape[0], weights.shape[1]

    def copy(ref, i):
        flip_big, flip_l, flip_x = keys[i]
        block = 4 * (big ^ flip_big) + 2 * (l ^ flip_l) + (x ^ flip_x)
        return pltpu.make_async_copy(
            ref.at[:, pl.ds(first_col, cols)],
            weights.at[pl.ds(pl.multiple_of(block * rows, 16), rows), :],
            sems.at[i],
        )

    for i in range(count):
        if len(refs) > count:
            pl.when(matched == 1)(copy(refs[i], i).start)
            pl.when(matched == 0)(copy(refs[count + i], i).start)
        else:
            copy(refs[i], i).start()
    for i in range(count):
        copy(refs[i], i).wait()


def query_kernel(keys, info, normed, bias, *rest):
    refs, (out, weights, sems) = rest[:-3], rest[-3:]
    fetch_weights(info, keys, refs, weights, sems)
    tile = 256
    for i in range(out.shape[0] // tile):
        rows = slice(i * tile, (i + 1) * tile)
        product = jnp.dot(normed[rows, :], weights[...], preferred_element_type=jnp.float32)
        out[rows, :] = (product + bias[...]).astype(jnp.bfloat16)


def keyval_kernel(first_col, keys, info, normed, pooled, bias, *rest):
    refs, (out, weights, sems) = rest[:-3], rest[-3:]
    fetch_weights(info, keys, refs, weights, sems, first_col)
    rows = normed.shape[0]
    cols = out.shape[1]
    product = jnp.dot(normed[...], weights[:, :cols], preferred_element_type=jnp.float32)
    out[:rows, :] = (product + bias[:, :cols]).astype(jnp.bfloat16)
    product = jnp.dot(pooled[...], weights[:, cols:], preferred_element_type=jnp.float32)
    out[rows:, :] = (product + bias[:, cols:]).astype(jnp.bfloat16)


def project(kernel, out_rows, out_cols, info, left, bias, own, copied):
    keys = tuple(own)
    width = left[0].shape[1]
    cols = bias.shape[0]
    return pl.pallas_call(
        functools.partial(kernel, keys),
        out_shape=jax.ShapeDtypeStruct((out_rows, out_cols), jnp.bfloat16),
        in_specs=[smem()] + [vmem()] * (len(left) + 1) + [hbm()] * (2 * len(keys)),
        out_specs=vmem(),
        scratch_shapes=[
            pltpu.VMEM((width, cols), jnp.bfloat16),
            pltpu.SemaphoreType.DMA((len(keys),)),
        ],
        compiler_params=params(),
        cost_estimate=pl.CostEstimate(
            flops=2 * out_rows * out_cols * width,
            bytes_accessed=2 * width * (out_rows + cols),
            transcendentals=0,
        ),
        name="project",
    )(info, *left, bias.reshape(1, -1), *[own[k] for k in keys], *[copied[k] for k in keys])


def attend_kernel(tokens, beacons, first_row, info, ratios, queries, pair, far_pair, *rest):
    beacon_refs, out = rest[:beacons], rest[beacons]
    place = 2 * info[7] + info[6]
    big = info[4]
    scale = 1.0 / math.sqrt(HEAD_DIM)
    stride = pair.shape[0] // 2
    slots = stride - tokens
    tile = min(256, tokens)

    def pieces(variant):
        full = []
        if variant in (1, 3):
            full.append((pair, stride))
        if variant in (2, 3):
            full += [(far_pair, 0), (far_pair, stride)]
        return full

    def score(rows, keys):
        return lax.dot_general(
            rows, keys, (((1,), (1,)), ((), ())), preferred_element_type=jnp.float32
        ) * scale

    def run(variant):
        for local_start in range(0, out.shape[0], tile):
            start = first_row + local_start
            rows = queries[start : start + tile, :]
            parts = []
            seen = start + tile
            scores = score(rows, pair[:seen, :HEAD_DIM])
            q_pos = start + lax.broadcasted_iota(jnp.int32, (tile, seen), 0)
            k_pos = lax.broadcasted_iota(jnp.int32, (tile, seen), 1)
            parts.append((jnp.where(k_pos <= q_pos, scores, -1e30), pair[:seen, HEAD_DIM:]))
            for ref, offset in pieces(variant):
                parts.append(
                    (
                        score(rows, ref[offset : offset + tokens, :HEAD_DIM]),
                        ref[offset : offset + tokens, HEAD_DIM:],
                    )
                )
            for m in range(beacons):
                source = big ^ (m + 1)
                count = beacon_refs[m].shape[0]
                live = jnp.where(source < big, tokens // ratios[source], 0)
                local = lax.broadcasted_iota(jnp.int32, (tile, count), 1) % slots
                scores = score(rows, beacon_refs[m][:, :HEAD_DIM])
                parts.append((jnp.where(local < live, scores, -1e30), beacon_refs[m][:, HEAD_DIM:]))
            top = functools.reduce(
                jnp.maximum, [jnp.max(s, axis=1, keepdims=True) for s, _ in parts]
            )
            total = jnp.zeros((tile, 1), jnp.float32)
            mixed = jnp.zeros((tile, HEAD_DIM), jnp.float32)
            for scores, values in parts:
                weights = jnp.exp(scores - top)
                total += jnp.sum(weights, axis=1, keepdims=True)
                mixed += jnp.dot(
                    weights.astype(jnp.bfloat16), values, preferred_element_type=jnp.float32
                )
            out[local_start : local_start + tile, :] = (mixed / total).astype(jnp.bfloat16)

    for variant in range(SPLIT):
        pl.when(place == variant)(functools.partial(run, variant))


def attend(first_row, row_count, info, ratios, queries, pair, far_pair, beacons):
    tokens, cols = queries.shape
    heads = cols // HEAD_DIM
    keys = 4 * tokens + sum(b.shape[0] for b in beacons)
    return pl.pallas_call(
        functools.partial(attend_kernel, tokens, len(beacons), first_row),
        grid=(heads,),
        out_shape=jax.ShapeDtypeStruct((row_count, cols), jnp.bfloat16),
        in_specs=[
            smem(),
            smem(),
            pl.BlockSpec((tokens, HEAD_DIM), lambda i: (0, i)),
            vmem(),
            vmem(),
        ]
        + [vmem()] * len(beacons),
        out_specs=pl.BlockSpec((row_count, HEAD_DIM), lambda i: (0, i)),
        compiler_params=params(),
        cost_estimate=pl.CostEstimate(
            flops=4 * row_count * keys * cols,
            bytes_accessed=4 * tokens * cols,
            transcendentals=row_count * keys * heads,
        ),
        name="attend",
    )(info, ratios, queries, pair, far_pair, *beacons)


def out_kernel(keys, info, attention, *rest):
    refs, (out, weights, sems) = rest[:-3], rest[-3:]
    fetch_weights(info, keys, refs, weights, sems)
    width = out.shape[3]
    for i in (1, 0):
        for j in (1, 0):
            group = 2 * (info[1] ^ j) + (info[7] ^ i)
            block = weights[pl.ds(pl.multiple_of(group * width, 16), width), :]
            out[i, j] = lax.dot_general(
                attention[...], block, (((1,), (1,)), ((), ())), preferred_element_type=jnp.float32
            ).astype(jnp.bfloat16)


def out_project(info, attention, pieces):
    tokens, depth = attention.shape
    keys = tuple(pieces)
    width = len(keys) * pieces[keys[0]].shape[0] // KVH
    return pl.pallas_call(
        functools.partial(out_kernel, keys),
        out_shape=jax.ShapeDtypeStruct((2, 2, tokens, width), jnp.bfloat16),
        in_specs=[smem(), vmem()] + [hbm()] * len(keys),
        out_specs=vmem(),
        scratch_shapes=[
            pltpu.VMEM((KVH * width, depth), jnp.bfloat16),
            pltpu.SemaphoreType.DMA((len(keys),)),
        ],
        compiler_params=params(),
        cost_estimate=pl.CostEstimate(
            flops=8 * tokens * width * depth, bytes_accessed=8 * width * depth, transcendentals=0
        ),
        name="out_project",
    )(info, attention, *[pieces[k] for k in keys])


def together(*values):
    return lax.optimization_barrier(values)


def on_device(
    hidden,
    norm_gain,
    query_weight,
    query_bias,
    keyval_weight,
    keyval_bias,
    beacon_weight,
    beacon_bias,
    out_weight,
    ratios,
):
    n_seq = lax.axis_size("seq")
    rows_dev = hidden.shape[0]
    half = rows_dev // 2
    seq_index = lax.axis_index("seq")
    head_index = lax.axis_index("head")
    big, l, x = seq_index // 4, (seq_index // 2) % 2, seq_index % 2
    y, c = head_index // 2, head_index % 2
    matched = c == l
    segment_ids = jnp.arange(ratios.shape[0], dtype=jnp.int32)
    own_ratio = jnp.sum(jnp.where(segment_ids == big, ratios, 0))
    inner = big != l
    info = jnp.stack(
        [
            matched.astype(jnp.int32),
            y,
            own_ratio,
            rows_dev // own_ratio,
            big,
            l,
            x,
            c,
        ]
    ).astype(jnp.int32)

    kv_cols = 2 * keyval_weight.shape[2]
    depth = keyval_weight.shape[0]
    query_cols = query_weight.shape[1]
    biases = jnp.concatenate([query_bias, keyval_bias.reshape(-1), beacon_bias.reshape(-1)])
    shard = jnp.concatenate(
        [
            query_weight,
            keyval_weight.reshape(depth, kv_cols),
            beacon_weight.reshape(depth, kv_cols),
        ],
        axis=1,
    )
    out_shard = out_weight.T

    def to_other_l(value):
        return send(value, n_seq, lambda big, l, x, y, c: (big, 1 - l, x, y, c) if c != l else None)

    def to_other_big(value, bit):
        return send(value, n_seq, lambda big, l, x, y, c: (big ^ bit, l, x, y, c) if c == l else None)

    def to_other_x(value):
        return send(value, n_seq, lambda big, l, x, y, c: (big, l, 1 - x, y, c) if c == l else None)

    def to_other_core(value):
        return send(value, n_seq, lambda big, l, x, y, c: (big, l, x, y, 1 - c) if c == l else None)

    own, copied = {(0, 0, 0): shard}, {}
    own[0, 1, 0] = to_other_l(shard)
    own[1, 0, 0] = to_other_big(shard, 1)
    own[0, 0, 1] = to_other_x(shard)
    own_half = lax.dynamic_slice_in_dim(hidden, y * half, half, 0)
    first = send(
        own_half, n_seq, lambda big, l, x, y, c: (big, 1 - l, x, y, 1 - c) if c != l else None
    )
    other_biases = send(biases, n_seq, lambda big, l, x, y, c: (big, l, x, y, 1 - c))
    biases = jnp.where(matched, biases, other_biases)
    copied[0, 0, 0] = to_other_core(shard)

    own[0, 1, 0], own[1, 0, 0], own[0, 0, 1] = together(own[0, 1, 0], own[1, 0, 0], own[0, 0, 1])
    own[1, 1, 0] = to_other_big(own[0, 1, 0], 1)
    own[0, 1, 1] = to_other_x(own[0, 1, 0])
    own[1, 0, 1] = to_other_x(own[1, 0, 0])
    for key in ((0, 1, 0), (1, 0, 0), (0, 0, 1)):
        copied[key] = to_other_core(own[key])

    own[1, 1, 0], own[0, 1, 1], own[1, 0, 1], first, out_shard = together(
        own[1, 1, 0], own[0, 1, 1], own[1, 0, 1], first, out_shard
    )
    second = send(first, n_seq, lambda big, l, x, y, c: (big, l, x, 1 - y, c) if c != l else None)
    own[1, 1, 1] = to_other_x(own[1, 1, 0])
    for key in ((1, 1, 0), (0, 1, 1), (1, 0, 1)):
        copied[key] = to_other_core(own[key])
    bit = 2
    while bit < n_seq // SPLIT:
        for key in list(own):
            new = (key[0] ^ bit, key[1], key[2])
            own[new] = to_other_big(own[key], bit)
            copied[new] = to_other_core(own[new])
        bit *= 2

    def swap_l(value):
        return send(value, n_seq, lambda big, l, x, y, c: (big, 1 - l, x, y, c))

    def swap_inner(value):
        return send(
            value, n_seq, lambda big, l, x, y, c: (1 - big, 1 - l, x, y, c) if big != l else None
        )

    def to_outer(value):
        return send(value, n_seq, lambda big, l, x, y, c: (big, 1 - l, x, y, c) if big != l else None)

    def swap_x(value):
        return send(value, n_seq, lambda big, l, x, y, c: (big, l, 1 - x, y, c))

    out_pieces = {(0, 0, 0): out_shard, (0, 1, 0): swap_l(out_shard)}
    if n_seq == 2 * SPLIT:
        middle_own = swap_inner(out_shard)
        own[1, 1, 1], out_pieces[0, 1, 0], middle_own = together(
            own[1, 1, 1], out_pieces[0, 1, 0], middle_own
        )
        middle_other = swap_inner(out_pieces[0, 1, 0])
        outer_own = to_outer(middle_own)
        out_pieces[0, 0, 1] = swap_x(out_shard)
        middle_other, outer_own, out_pieces[0, 0, 1] = together(
            middle_other, outer_own, out_pieces[0, 0, 1]
        )
        outer_other = to_outer(middle_other)
        out_pieces[1, 1, 0] = jnp.where(inner, middle_own, outer_other)
        out_pieces[1, 0, 0] = jnp.where(inner, middle_other, outer_own)
    else:
        bit = 1
        while bit < n_seq // SPLIT:
            for key in list(out_pieces):
                out_pieces[key[0] ^ bit, key[1], 0] = send(
                    out_pieces[key], n_seq, lambda big, l, x, y, c: (big ^ bit, l, x, y, c)
                )
            bit *= 2
    for key in list(out_pieces):
        if (key[0], key[1], 1) not in out_pieces:
            out_pieces[key[0], key[1], 1] = swap_x(out_pieces[key])
    copied[1, 1, 1] = to_other_core(own[1, 1, 1])
    if n_seq > 2 * SPLIT:
        copied = {key: copied[key] for key in own}

    normed, pooled = norm_and_pool(info, hidden, first, second, norm_gain)
    slots_dev = rows_dev // R_MIN
    keyval = project(
        functools.partial(keyval_kernel, query_cols),
        rows_dev + slots_dev,
        kv_cols,
        info,
        [normed, pooled],
        biases[query_cols:],
        own,
        copied,
    )
    beside = send(keyval, n_seq, lambda big, l, x, y, c: (big, l, 1 - x, y, c))
    pair = jnp.concatenate([keyval, beside], axis=0)
    far_pair = send(pair, n_seq, lambda big, l, x, y, c: (big, l, x, y, 1 - c))
    stride = rows_dev + slots_dev
    beacons = [
        jnp.concatenate(
            [
                pair[rows_dev:stride],
                pair[stride + rows_dev :],
                far_pair[rows_dev:stride],
                far_pair[stride + rows_dev :],
            ],
            axis=0,
        )
    ]
    bit = 1
    while bit < n_seq // SPLIT:
        beacons += [
            send(piece, n_seq, lambda big, l, x, y, c: (big ^ bit, l, x, y, c)) for piece in beacons
        ]
        bit *= 2
    query = project(
        query_kernel,
        rows_dev,
        query_cols,
        info,
        [normed],
        biases[:query_cols],
        own,
        copied,
    )
    parts = 2
    part = rows_dev // parts
    results = []
    for i in range(parts):
        attention = attend(i * part, part, info, ratios, query, pair, far_pair, beacons[1:])
        swapped = send(
            attention, n_seq, lambda big, l, x, y, c: (big, 1 - l, x, y, 1 - c) if c != l else None
        )
        attention = jnp.where(matched, attention, swapped)
        partial = out_project(info, attention, out_pieces)
        from_core = send(partial[1], n_seq, lambda big, l, x, y, c: (big, l, x, y, 1 - c))
        sums = partial[0].astype(jnp.float32) + from_core.astype(jnp.float32)
        from_y = send(
            sums[1].astype(jnp.bfloat16), n_seq, lambda big, l, x, y, c: (big, l, x, 1 - y, c)
        )
        results.append((sums[0] + from_y.astype(jnp.float32)).astype(jnp.bfloat16))
    return jnp.concatenate(results, axis=0)


def solution(mesh):
    return jax.shard_map(
        on_device,
        mesh=mesh,
        in_specs=(
            P("seq", None),
            P(),
            P("seq", "head"),
            P("head"),
            P("seq", None, "head"),
            P(None, "head"),
            P("seq", None, "head"),
            P(None, "head"),
            P("head", "seq"),
            P(),
        ),
        out_specs=P("seq", "head"),
        check_vma=False,
    )
```

```python
import functools
import math

import jax
import jax.numpy as jnp
from jax import lax
from jax.experimental import pallas as pl
from jax.experimental.pallas import tpu as pltpu
from jax.sharding import PartitionSpec as P

QH = 28
KVH = 4
HEAD_DIM = 128
SPLIT = 4
R_MIN = 8
AXES = ("seq", "head")
VMEM_LIMIT = 56 * 1024 * 1024


def params():
    return pltpu.CompilerParams(vmem_limit_bytes=VMEM_LIMIT)


def vmem():
    return pl.BlockSpec(memory_space=pltpu.VMEM)


def smem():
    return pl.BlockSpec(memory_space=pltpu.SMEM)


def hbm():
    return pl.BlockSpec(memory_space=pl.ANY)


def moves(n_seq, rule):
    pairs = []
    for s in range(n_seq):
        for h in range(KVH):
            target = rule(s >> 2, (s >> 1) & 1, s & 1, h >> 1, h & 1)
            if target is not None:
                big, l, x, y, c = target
                pairs.append((s * KVH + h, (4 * big + 2 * l + x) * KVH + 2 * y + c))
    return pairs


def send(value, n_seq, rule):
    return lax.ppermute(value, AXES, moves(n_seq, rule))


def norm_kernel(info, hidden, first, second, gain, normed, pooled, buf, sems):
    rows = hidden.shape[0]
    half = rows // 2
    tiles = sems.shape[0]
    tile = rows // tiles
    matched, y_bit, ratio = info[0], info[1], info[2]

    def land(i):
        return buf.at[pl.ds(i * tile, tile), :]

    for i in range(tiles):

        @pl.when(matched == 1)
        def _():
            pltpu.make_async_copy(hidden.at[pl.ds(i * tile, tile), :], land(i), sems.at[i]).start()

        upper = (i * tile) // half
        local = pl.ds(i * tile - upper * half, tile)

        @pl.when((matched == 0) & (y_bit == upper))
        def _():
            pltpu.make_async_copy(first.at[local, :], land(i), sems.at[i]).start()

        @pl.when((matched == 0) & (y_bit != upper))
        def _():
            pltpu.make_async_copy(second.at[local, :], land(i), sems.at[i]).start()

    scale = gain[...]
    for i in range(tiles):
        pltpu.make_async_copy(hidden.at[pl.ds(i * tile, tile), :], land(i), sems.at[i]).wait()
        floats = buf[i * tile : (i + 1) * tile, :].astype(jnp.float32)
        mean = jnp.mean(floats * floats, axis=1, keepdims=True)
        normed[i * tile : (i + 1) * tile, :] = (floats * lax.rsqrt(mean + 1e-06) * scale).astype(
            jnp.bfloat16
        )
    slots = pooled.shape[0]
    token = lax.broadcasted_iota(jnp.int32, (slots, rows), 1)
    slot = lax.broadcasted_iota(jnp.int32, (slots, rows), 0)
    member = (
        (token >= slot * ratio) & (token < (slot + 1) * ratio) & (slot < info[3])
    ).astype(jnp.float32).astype(jnp.bfloat16)
    total = jnp.dot(member, normed[...], preferred_element_type=jnp.float32)
    pooled[...] = (total / ratio.astype(jnp.float32)).astype(jnp.bfloat16)


def norm_and_pool(info, hidden, first, second, gain):
    rows, width = hidden.shape
    tiles = 8
    return pl.pallas_call(
        norm_kernel,
        out_shape=(
            jax.ShapeDtypeStruct((rows, width), jnp.bfloat16),
            jax.ShapeDtypeStruct((rows // R_MIN, width), jnp.bfloat16),
        ),
        in_specs=[smem(), hbm(), hbm(), hbm(), vmem()],
        out_specs=(vmem(), vmem()),
        scratch_shapes=[pltpu.VMEM((rows, width), jnp.bfloat16), pltpu.SemaphoreType.DMA((tiles,))],
        compiler_params=params(),
        cost_estimate=pl.CostEstimate(
            flops=2 * rows * rows // R_MIN * width, bytes_accessed=4 * rows * width, transcendentals=0
        ),
        name="norm_pool",
    )(info, hidden, first, second, gain)


def block_of(info, key):
    return 4 * (info[4] ^ key[0]) + 2 * (info[5] ^ key[1]) + (info[6] ^ key[2])


def chunk_blocks(rows):
    blocks = 2
    while blocks * rows % 128:
        blocks *= 2
    return blocks


def load_chunks(info, keys, refs, weights, sems, normed, left, left_sems, first_col):
    count = len(keys)
    rows, cols = refs[0].shape[0], weights.shape[2]
    blocks = chunk_blocks(rows)
    chunks = count // blocks
    flips = [4 * key[0] + 2 * key[1] + key[2] for key in keys]

    def chunk_of(k):
        return block_of(info, (0, 0, 0)) // blocks ^ k

    def members(k):
        return [i for i in range(count) if flips[i] // blocks == k]

    def piece(ref, i, k):
        spot = block_of(info, keys[i]) % blocks * rows
        return pltpu.make_async_copy(
            ref.at[:, pl.ds(first_col, cols)],
            weights.at[k, pl.ds(pl.multiple_of(spot, 16), rows), :],
            sems.at[i],
        )

    def columns(k):
        start = pl.multiple_of(chunk_of(k) * (blocks * rows), 128)
        return pltpu.make_async_copy(
            normed.at[:, pl.ds(start, blocks * rows)], left.at[k], left_sems.at[k]
        )

    for k in range(chunks):
        columns(k).start()
        for i in members(k):
            pl.when(info[0] == 1)(piece(refs[i], i, k).start)
            pl.when(info[0] == 0)(piece(refs[count + i], i, k).start)

    def wait(k):
        columns(k).wait()
        for i in members(k):
            piece(refs[i], i, k).wait()

    return chunks, wait, chunk_of


def query_kernel(first_col, keys, info, normed, bias, *rest):
    refs, (out, weights, sems, left, left_sems, total) = rest[:-6], rest[-6:]
    chunks, wait, _ = load_chunks(
        info, keys, refs, weights, sems, normed, left, left_sems, first_col
    )
    for k in range(chunks):
        wait(k)
        product = jnp.dot(left[k], weights[k], preferred_element_type=jnp.float32)
        if k == 0:
            total[...] = product + bias[...]
        elif k < chunks - 1:
            total[...] += product
        else:
            out[...] = (total[...] + product).astype(jnp.bfloat16)


def keyval_kernel(first_col, keys, info, normed, pooled, bias, *rest):
    refs, (out, weights, sems, left, left_sems, total) = rest[:-6], rest[-6:]
    chunks, wait, chunk_of = load_chunks(
        info, keys, refs, weights, sems, normed, left, left_sems, first_col
    )
    tokens, depth = normed.shape[0], weights.shape[1]
    cols = out.shape[1]
    for k in range(chunks):
        wait(k)
        slots = pooled[:, pl.ds(pl.multiple_of(chunk_of(k) * depth, 128), depth)]
        product = jnp.dot(left[k], weights[k, :, :cols], preferred_element_type=jnp.float32)
        beacon = jnp.dot(slots, weights[k, :, cols:], preferred_element_type=jnp.float32)
        if k == 0:
            total[:tokens, :] = product + bias[:, :cols]
            total[tokens:, :] = beacon + bias[:, cols:]
        elif k < chunks - 1:
            total[:tokens, :] += product
            total[tokens:, :] += beacon
        else:
            out[:tokens, :] = (total[:tokens, :] + product).astype(jnp.bfloat16)
            out[tokens:, :] = (total[tokens:, :] + beacon).astype(jnp.bfloat16)


def project(kernel, out_rows, out_cols, info, left, bias, own, copied):
    keys = tuple(own)
    rows = own[keys[0]].shape[0]
    blocks = chunk_blocks(rows)
    tokens, width = left[0].shape
    cols = bias.shape[0]
    chunks = len(keys) // blocks
    return pl.pallas_call(
        functools.partial(kernel, keys),
        out_shape=jax.ShapeDtypeStruct((out_rows, out_cols), jnp.bfloat16),
        in_specs=[smem(), hbm()] + [vmem()] * len(left) + [hbm()] * (2 * len(keys)),
        out_specs=vmem(),
        scratch_shapes=[
            pltpu.VMEM((chunks, blocks * rows, cols), jnp.bfloat16),
            pltpu.SemaphoreType.DMA((len(keys),)),
            pltpu.VMEM((chunks, tokens, blocks * rows), jnp.bfloat16),
            pltpu.SemaphoreType.DMA((chunks,)),
            pltpu.VMEM((out_rows, out_cols), jnp.float32),
        ],
        compiler_params=params(),
        cost_estimate=pl.CostEstimate(
            flops=2 * out_rows * out_cols * width,
            bytes_accessed=2 * width * (out_rows + cols),
            transcendentals=0,
        ),
        name="project",
    )(info, *left, bias.reshape(1, -1), *[own[k] for k in keys], *[copied[k] for k in keys])


def attend_kernel(tokens, slots, beacons, first_row, info, ratios, queries, *rest):
    pair, beside, across, corner = rest[:4]
    beacon_refs, out = rest[4 : 4 + beacons], rest[4 + beacons]
    place = 2 * info[7] + info[6]
    big = info[4]
    scale = 1.0 / math.sqrt(HEAD_DIM)
    tile = min(256, tokens)

    def pieces(variant):
        full = []
        if variant in (1, 3):
            full.append(beside)
        if variant in (2, 3):
            full += [across, corner]
        return full

    def score(rows, keys):
        return lax.dot_general(
            rows, keys, (((1,), (1,)), ((), ())), preferred_element_type=jnp.float32
        ) * scale

    def run(variant):
        for local_start in range(0, out.shape[0], tile):
            start = first_row + local_start
            rows = queries[start : start + tile, :]
            parts = []
            seen = start + tile
            scores = score(rows, pair[:seen, :HEAD_DIM])
            q_pos = start + lax.broadcasted_iota(jnp.int32, (tile, seen), 0)
            k_pos = lax.broadcasted_iota(jnp.int32, (tile, seen), 1)
            parts.append((jnp.where(k_pos <= q_pos, scores, -1e30), pair[:seen, HEAD_DIM:]))
            for ref in pieces(variant):
                parts.append((score(rows, ref[:tokens, :HEAD_DIM]), ref[:tokens, HEAD_DIM:]))
            for m in range(beacons):
                source = big ^ (m + 1)
                count = beacon_refs[m].shape[0]
                live = jnp.where(source < big, tokens // ratios[source], 0)
                local = lax.broadcasted_iota(jnp.int32, (tile, count), 1) % slots
                scores = score(rows, beacon_refs[m][:, :HEAD_DIM])
                parts.append((jnp.where(local < live, scores, -1e30), beacon_refs[m][:, HEAD_DIM:]))
            top = functools.reduce(
                jnp.maximum, [jnp.max(s, axis=1, keepdims=True) for s, _ in parts]
            )
            total = jnp.zeros((tile, 1), jnp.float32)
            mixed = jnp.zeros((tile, HEAD_DIM), jnp.float32)
            for scores, values in parts:
                weights = jnp.exp(scores - top)
                total += jnp.sum(weights, axis=1, keepdims=True)
                mixed += jnp.dot(
                    weights.astype(jnp.bfloat16), values, preferred_element_type=jnp.float32
                )
            out[local_start : local_start + tile, :] = (mixed / total).astype(jnp.bfloat16)

    for variant in range(SPLIT):
        pl.when(place == variant)(functools.partial(run, variant))


def attend(first_row, row_count, info, ratios, queries, keyvals, beacons):
    tokens, cols = queries.shape
    slots = keyvals[0].shape[0] - tokens
    heads = cols // HEAD_DIM
    keys = 4 * tokens + sum(b.shape[0] for b in beacons)
    return pl.pallas_call(
        functools.partial(attend_kernel, tokens, slots, len(beacons), first_row),
        grid=(heads,),
        out_shape=jax.ShapeDtypeStruct((row_count, cols), jnp.bfloat16),
        in_specs=[smem(), smem(), pl.BlockSpec((tokens, HEAD_DIM), lambda i: (0, i))]
        + [vmem()] * (len(keyvals) + len(beacons)),
        out_specs=pl.BlockSpec((row_count, HEAD_DIM), lambda i: (0, i)),
        compiler_params=params(),
        cost_estimate=pl.CostEstimate(
            flops=4 * row_count * keys * cols,
            bytes_accessed=4 * tokens * cols,
            transcendentals=row_count * keys * heads,
        ),
        name="attend",
    )(info, ratios, queries, *keyvals, *beacons)


def out_kernel(keys, info, attention, *rest):
    refs, (away, kept, weights, sems) = rest[:-4], rest[-4:]
    rows = refs[0].shape[0]
    width = kept.shape[2]
    per_group = width // rows

    for i, key in enumerate(keys):
        block = block_of(info, key)
        group = (block // per_group) ^ (2 * info[1] + info[7])
        spot = pl.multiple_of((block % per_group) * rows, 16)
        pltpu.make_async_copy(
            refs[i], weights.at[group, pl.ds(spot, rows), :], sems.at[group]
        ).start()
    for out, j, group in ((away, 1, 3), (away, 0, 1), (kept, 1, 2), (kept, 0, 0)):
        pltpu.make_async_copy(weights.at[group], weights.at[group], sems.at[group]).wait()
        out[j] = lax.dot_general(
            attention[...],
            weights[group],
            (((1,), (1,)), ((), ())),
            preferred_element_type=jnp.float32,
        ).astype(jnp.bfloat16)


def out_project(info, attention, pieces):
    tokens, depth = attention.shape
    keys = tuple(pieces)
    width = len(keys) * pieces[keys[0]].shape[0] // KVH
    shape = jax.ShapeDtypeStruct((2, tokens, width), jnp.bfloat16)
    return pl.pallas_call(
        functools.partial(out_kernel, keys),
        out_shape=(shape, shape),
        in_specs=[smem(), vmem()] + [hbm()] * len(keys),
        out_specs=(vmem(), vmem()),
        scratch_shapes=[
            pltpu.VMEM((KVH, width, depth), jnp.bfloat16),
            pltpu.SemaphoreType.DMA((KVH,)),
        ],
        compiler_params=params(),
        cost_estimate=pl.CostEstimate(
            flops=8 * tokens * width * depth, bytes_accessed=8 * width * depth, transcendentals=0
        ),
        name="out_project",
    )(info, attention, *[pieces[k] for k in keys])


def together(*values):
    return lax.optimization_barrier(values)


def on_device(
    hidden,
    norm_gain,
    query_weight,
    query_bias,
    keyval_weight,
    keyval_bias,
    beacon_weight,
    beacon_bias,
    out_weight,
    ratios,
):
    n_seq = lax.axis_size("seq")
    rows_dev = hidden.shape[0]
    half = rows_dev // 2
    seq_index = lax.axis_index("seq")
    head_index = lax.axis_index("head")
    big, l, x = seq_index // 4, (seq_index // 2) % 2, seq_index % 2
    y, c = head_index // 2, head_index % 2
    matched = c == l
    segment_ids = jnp.arange(ratios.shape[0], dtype=jnp.int32)
    own_ratio = jnp.sum(jnp.where(segment_ids == big, ratios, 0))
    inner = big != l
    info = jnp.stack(
        [
            matched.astype(jnp.int32),
            y,
            own_ratio,
            rows_dev // own_ratio,
            big,
            l,
            x,
            c,
        ]
    ).astype(jnp.int32)

    kv_cols = 2 * keyval_weight.shape[2]
    depth = keyval_weight.shape[0]
    query_cols = query_weight.shape[1]
    biases = jnp.concatenate([query_bias, keyval_bias.reshape(-1), beacon_bias.reshape(-1)])
    shard = jnp.concatenate(
        [
            query_weight,
            keyval_weight.reshape(depth, kv_cols),
            beacon_weight.reshape(depth, kv_cols),
        ],
        axis=1,
    )
    out_shard = out_weight.T

    def to_other_l(value):
        return send(value, n_seq, lambda big, l, x, y, c: (big, 1 - l, x, y, c) if c != l else None)

    def to_other_big(value, bit):
        return send(value, n_seq, lambda big, l, x, y, c: (big ^ bit, l, x, y, c) if c == l else None)

    def to_other_x(value):
        return send(value, n_seq, lambda big, l, x, y, c: (big, l, 1 - x, y, c) if c == l else None)

    def to_other_core(value):
        return send(value, n_seq, lambda big, l, x, y, c: (big, l, x, y, 1 - c) if c == l else None)

    def swap_l(value):
        return send(value, n_seq, lambda big, l, x, y, c: (big, 1 - l, x, y, c))

    def swap_big(value, bit):
        return send(value, n_seq, lambda big, l, x, y, c: (big ^ bit, l, x, y, c))

    def swap_inner(value):
        return send(
            value, n_seq, lambda big, l, x, y, c: (1 - big, 1 - l, x, y, c) if big != l else None
        )

    def to_outer(value):
        return send(value, n_seq, lambda big, l, x, y, c: (big, 1 - l, x, y, c) if big != l else None)

    def swap_x(value):
        return send(value, n_seq, lambda big, l, x, y, c: (big, l, 1 - x, y, c))

    own, copied = {(0, 0, 0): shard}, {}
    own_half = lax.dynamic_slice_in_dim(hidden, y * half, half, 0)
    first = send(
        own_half, n_seq, lambda big, l, x, y, c: (big, 1 - l, x, y, 1 - c) if c != l else None
    )
    own[0, 1, 0] = to_other_l(shard)
    own[1, 0, 0] = to_other_big(shard, 1)
    own[0, 0, 1] = to_other_x(shard)
    other_biases = send(biases, n_seq, lambda big, l, x, y, c: (big, l, x, y, 1 - c))
    biases = jnp.where(matched, biases, other_biases)
    gain = norm_gain.reshape(1, -1)
    own[0, 1, 0], own[1, 0, 0], own[0, 0, 1], biases, gain, info = together(
        own[0, 1, 0], own[1, 0, 0], own[0, 0, 1], biases, gain, info
    )
    own[1, 1, 0] = to_other_big(own[0, 1, 0], 1)
    own[0, 1, 1] = to_other_x(own[0, 1, 0])
    own[1, 0, 1] = to_other_x(own[1, 0, 0])
    keys = ((0, 0, 0), (0, 1, 0), (1, 0, 0), (0, 0, 1))
    for key in keys:
        copied[key] = to_other_core(own[key])
    (
        own[1, 1, 0],
        own[0, 1, 1],
        own[1, 0, 1],
        first,
        copied[0, 0, 0],
        copied[0, 1, 0],
        copied[1, 0, 0],
        copied[0, 0, 1],
    ) = together(
        own[1, 1, 0], own[0, 1, 1], own[1, 0, 1], first, *[copied[key] for key in keys]
    )
    own[1, 1, 1] = to_other_x(own[1, 1, 0])
    second = send(first, n_seq, lambda big, l, x, y, c: (big, l, x, 1 - y, c) if c != l else None)
    keys = ((1, 1, 0), (0, 1, 1), (1, 0, 1))
    for key in keys:
        copied[key] = to_other_core(own[key])
    copied[1, 1, 0], copied[0, 1, 1], copied[1, 0, 1], out_shard = together(
        *[copied[key] for key in keys], out_shard
    )
    outs = {(0, 0, 0): out_shard, (0, 1, 0): swap_l(out_shard)}
    two_segments = n_seq == 2 * SPLIT
    middle_own = swap_inner(out_shard) if two_segments else out_shard
    outs[0, 0, 1] = swap_x(out_shard)
    bit = 2
    while bit < n_seq // SPLIT:
        for key in list(own):
            new = (key[0] ^ bit, key[1], key[2])
            own[new] = to_other_big(own[key], bit)
            copied[new] = to_other_core(own[new])
        bit *= 2

    normed, pooled = norm_and_pool(info, hidden, first, second, gain)
    if two_segments:
        normed, middle_own, outs[0, 1, 0], outs[0, 0, 1], own[1, 1, 1] = together(
            normed, middle_own, outs[0, 1, 0], outs[0, 0, 1], own[1, 1, 1]
        )
        middle_other = swap_inner(outs[0, 1, 0])
        outer_own = to_outer(middle_own)
        outs[0, 1, 1] = swap_x(outs[0, 1, 0])
    copied[1, 1, 1] = to_other_core(own[1, 1, 1])
    slots_dev = rows_dev // R_MIN
    copied = {key: copied[key] for key in own}
    keyval = project(
        functools.partial(keyval_kernel, query_cols),
        rows_dev + slots_dev,
        kv_cols,
        info,
        [normed, pooled],
        biases[query_cols:],
        own,
        copied,
    )
    beside = send(keyval, n_seq, lambda big, l, x, y, c: (big, l, 1 - x, y, c))
    across = send(keyval, n_seq, lambda big, l, x, y, c: (big, l, x, y, 1 - c))
    normed, keyval = together(normed, keyval)
    query = project(
        functools.partial(query_kernel, 0),
        rows_dev,
        query_cols,
        info,
        [normed],
        biases[:query_cols],
        own,
        copied,
    )
    query, beside, across = together(query, beside, across)
    corner = send(beside, n_seq, lambda big, l, x, y, c: (big, l, x, y, 1 - c))
    beacons = [
        jnp.concatenate([piece[rows_dev:] for piece in (keyval, beside, across, corner)], axis=0)
    ]
    bit = 1
    while bit < n_seq // SPLIT:
        beacons += [swap_big(piece, bit) for piece in beacons]
        bit *= 2
    beacons = beacons[1:]
    if two_segments:
        query, middle_other, outer_own, outs[0, 1, 1] = together(
            query, middle_other, outer_own, outs[0, 1, 1]
        )
        outer_other = to_outer(middle_other)
        outs[1, 0, 0] = jnp.where(inner, middle_other, outer_own)
        outs[1, 0, 1] = swap_x(outs[1, 0, 0])
    else:
        bit = 1
        while bit < n_seq // SPLIT:
            for key in list(outs):
                if key[2] == 0:
                    outs[key[0] ^ bit, key[1], 0] = swap_big(outs[key], bit)
            bit *= 2
        for key in list(outs):
            if (key[0], key[1], 1) not in outs:
                outs[key[0], key[1], 1] = swap_x(outs[key])

    def attend_rows(first_row, row_count):
        return attend(
            first_row, row_count, info, ratios, query, [keyval, beside, across, corner], beacons
        )

    def swap_back(value):
        return send(
            value, n_seq, lambda big, l, x, y, c: (big, 1 - l, x, y, 1 - c) if c != l else None
        )

    def swap_core(value):
        return send(value, n_seq, lambda big, l, x, y, c: (big, l, x, y, 1 - c))

    def swap_y(value):
        return send(value, n_seq, lambda big, l, x, y, c: (big, l, x, 1 - y, c))

    def add(kept, from_core):
        sums = kept.astype(jnp.float32) + from_core.astype(jnp.float32)
        return sums[0], sums[1].astype(jnp.bfloat16)

    part = rows_dev // 2
    early = attend_rows(0, part)
    if two_segments:
        early, outer_other, outs[1, 0, 1] = together(early, outer_other, outs[1, 0, 1])
        outs[1, 1, 0] = jnp.where(inner, middle_own, outer_other)
        outs[1, 1, 1] = swap_x(outs[1, 1, 0])
    early_swapped = swap_back(early)
    query, early = together(query, early)
    late = attend_rows(part, part)
    late, early, early_swapped = together(late, early, early_swapped)
    late_swapped = swap_back(late)
    early_away, early_kept = out_project(info, jnp.where(matched, early, early_swapped), outs)
    early_away, early_kept, late, late_swapped = together(
        early_away, early_kept, late, late_swapped
    )
    early_near, early_far = add(early_kept, swap_core(early_away))
    late = jnp.where(matched, late, late_swapped)
    late, early_near, early_far = together(late, early_near, early_far)
    early_from_y = swap_y(early_far)
    late_away, late_kept = out_project(info, late, outs)
    late_away, late_kept, early_from_y = together(late_away, late_kept, early_from_y)
    late_near, late_far = add(late_kept, swap_core(late_away))
    results = [(early_near, early_from_y), (late_near, swap_y(late_far))]
    return jnp.concatenate(
        [(near + from_y.astype(jnp.float32)).astype(jnp.bfloat16) for near, from_y in results], axis=0
    )


def solution(mesh):
    return jax.shard_map(
        on_device,
        mesh=mesh,
        in_specs=(
            P("seq", None),
            P(),
            P("seq", "head"),
            P("head"),
            P("seq", None, "head"),
            P(None, "head"),
            P("seq", None, "head"),
            P(None, "head"),
            P("head", "seq"),
            P(),
        ),
        out_specs=P("seq", "head"),
        check_vma=False,
    )
```

```python
import functools
import math

import jax
import jax.numpy as jnp
from jax import lax
from jax.experimental import pallas as pl
from jax.experimental.pallas import tpu as pltpu
from jax.sharding import PartitionSpec as P

QH = 28
KVH = 4
HEAD_DIM = 128
SPLIT = 4
R_MIN = 8
AXES = ("seq", "head")
VMEM_LIMIT = 56 * 1024 * 1024


def params():
    return pltpu.CompilerParams(vmem_limit_bytes=VMEM_LIMIT)


def vmem():
    return pl.BlockSpec(memory_space=pltpu.VMEM)


def smem():
    return pl.BlockSpec(memory_space=pltpu.SMEM)


def hbm():
    return pl.BlockSpec(memory_space=pl.ANY)


def moves(n_seq, rule):
    pairs = []
    for s in range(n_seq):
        for h in range(KVH):
            target = rule(s >> 2, (s >> 1) & 1, s & 1, h >> 1, h & 1)
            if target is not None:
                big, l, x, y, c = target
                pairs.append((s * KVH + h, (4 * big + 2 * l + x) * KVH + 2 * y + c))
    return pairs


def send(value, n_seq, rule):
    return lax.ppermute(value, AXES, moves(n_seq, rule))


def norm_kernel(info, hidden, first, second, gain, normed, pooled, buf, sems):
    rows = hidden.shape[0]
    half = rows // 2
    tiles = sems.shape[0]
    tile = rows // tiles
    matched, y_bit, ratio = info[0], info[1], info[2]

    def land(i):
        return buf.at[pl.ds(i * tile, tile), :]

    for i in range(tiles):

        @pl.when(matched == 1)
        def _():
            pltpu.make_async_copy(hidden.at[pl.ds(i * tile, tile), :], land(i), sems.at[i]).start()

        upper = (i * tile) // half
        local = pl.ds(i * tile - upper * half, tile)

        @pl.when((matched == 0) & (y_bit == upper))
        def _():
            pltpu.make_async_copy(first.at[local, :], land(i), sems.at[i]).start()

        @pl.when((matched == 0) & (y_bit != upper))
        def _():
            pltpu.make_async_copy(second.at[local, :], land(i), sems.at[i]).start()

    scale = gain[...]
    for i in range(tiles):
        pltpu.make_async_copy(hidden.at[pl.ds(i * tile, tile), :], land(i), sems.at[i]).wait()
        floats = buf[i * tile : (i + 1) * tile, :].astype(jnp.float32)
        mean = jnp.mean(floats * floats, axis=1, keepdims=True)
        normed[i * tile : (i + 1) * tile, :] = (floats * lax.rsqrt(mean + 1e-06) * scale).astype(
            jnp.bfloat16
        )
    slots = pooled.shape[0]
    token = lax.broadcasted_iota(jnp.int32, (slots, rows), 1)
    slot = lax.broadcasted_iota(jnp.int32, (slots, rows), 0)
    member = (
        (token >= slot * ratio) & (token < (slot + 1) * ratio) & (slot < info[3])
    ).astype(jnp.float32).astype(jnp.bfloat16)
    total = jnp.dot(member, normed[...], preferred_element_type=jnp.float32)
    pooled[...] = (total / ratio.astype(jnp.float32)).astype(jnp.bfloat16)


def norm_and_pool(info, hidden, first, second, gain):
    rows, width = hidden.shape
    tiles = 8
    return pl.pallas_call(
        norm_kernel,
        out_shape=(
            jax.ShapeDtypeStruct((rows, width), jnp.bfloat16),
            jax.ShapeDtypeStruct((rows // R_MIN, width), jnp.bfloat16),
        ),
        in_specs=[smem(), hbm(), hbm(), hbm(), vmem()],
        out_specs=(vmem(), vmem()),
        scratch_shapes=[pltpu.VMEM((rows, width), jnp.bfloat16), pltpu.SemaphoreType.DMA((tiles,))],
        compiler_params=params(),
        cost_estimate=pl.CostEstimate(
            flops=2 * rows * rows // R_MIN * width, bytes_accessed=4 * rows * width, transcendentals=0
        ),
        name="norm_pool",
    )(info, hidden, first, second, gain)


def block_of(info, key):
    return 4 * (info[4] ^ key[0]) + 2 * (info[5] ^ key[1]) + (info[6] ^ key[2])


def chunk_blocks(rows):
    blocks = 2
    while blocks * rows % 128:
        blocks *= 2
    return blocks


def load_chunks(info, keys, refs, weights, sems, normed, left, left_sems, first_col):
    count = len(keys)
    rows, cols = refs[0].shape[0], weights.shape[2]
    blocks = chunk_blocks(rows)
    chunks = count // blocks
    flips = [4 * key[0] + 2 * key[1] + key[2] for key in keys]

    def chunk_of(k):
        return block_of(info, (0, 0, 0)) // blocks ^ k

    def members(k):
        return [i for i in range(count) if flips[i] // blocks == k]

    def piece(ref, i, k):
        spot = block_of(info, keys[i]) % blocks * rows
        return pltpu.make_async_copy(
            ref.at[:, pl.ds(first_col, cols)],
            weights.at[k, pl.ds(pl.multiple_of(spot, 16), rows), :],
            sems.at[i],
        )

    def columns(k):
        start = pl.multiple_of(chunk_of(k) * (blocks * rows), 128)
        return pltpu.make_async_copy(
            normed.at[:, pl.ds(start, blocks * rows)], left.at[k], left_sems.at[k]
        )

    for k in range(chunks):
        columns(k).start()
        for i in members(k):
            pl.when(info[0] == 1)(piece(refs[i], i, k).start)
            pl.when(info[0] == 0)(piece(refs[count + i], i, k).start)

    def wait(k):
        columns(k).wait()
        for i in members(k):
            piece(refs[i], i, k).wait()

    return chunks, wait, chunk_of


def query_kernel(first_col, keys, info, normed, bias, *rest):
    refs, (out, weights, sems, left, left_sems, total) = rest[:-6], rest[-6:]
    chunks, wait, _ = load_chunks(
        info, keys, refs, weights, sems, normed, left, left_sems, first_col
    )
    for k in range(chunks):
        wait(k)
        product = jnp.dot(left[k], weights[k], preferred_element_type=jnp.float32)
        if k == 0:
            total[...] = product + bias[...]
        elif k < chunks - 1:
            total[...] += product
        else:
            out[...] = (total[...] + product).astype(jnp.bfloat16)


def keyval_kernel(first_col, keys, info, normed, pooled, bias, *rest):
    refs, (out, weights, sems, left, left_sems, total) = rest[:-6], rest[-6:]
    chunks, wait, chunk_of = load_chunks(
        info, keys, refs, weights, sems, normed, left, left_sems, first_col
    )
    tokens, depth = normed.shape[0], weights.shape[1]
    cols = out.shape[1]
    for k in range(chunks):
        wait(k)
        slots = pooled[:, pl.ds(pl.multiple_of(chunk_of(k) * depth, 128), depth)]
        product = jnp.dot(left[k], weights[k, :, :cols], preferred_element_type=jnp.float32)
        beacon = jnp.dot(slots, weights[k, :, cols:], preferred_element_type=jnp.float32)
        if k == 0:
            total[:tokens, :] = product + bias[:, :cols]
            total[tokens:, :] = beacon + bias[:, cols:]
        elif k < chunks - 1:
            total[:tokens, :] += product
            total[tokens:, :] += beacon
        else:
            out[:tokens, :] = (total[:tokens, :] + product).astype(jnp.bfloat16)
            out[tokens:, :] = (total[tokens:, :] + beacon).astype(jnp.bfloat16)


def project(kernel, out_rows, out_cols, info, left, bias, own, copied):
    keys = tuple(own)
    rows = own[keys[0]].shape[0]
    blocks = chunk_blocks(rows)
    tokens, width = left[0].shape
    cols = bias.shape[0]
    chunks = len(keys) // blocks
    return pl.pallas_call(
        functools.partial(kernel, keys),
        out_shape=jax.ShapeDtypeStruct((out_rows, out_cols), jnp.bfloat16),
        in_specs=[smem(), hbm()] + [vmem()] * len(left) + [hbm()] * (2 * len(keys)),
        out_specs=vmem(),
        scratch_shapes=[
            pltpu.VMEM((chunks, blocks * rows, cols), jnp.bfloat16),
            pltpu.SemaphoreType.DMA((len(keys),)),
            pltpu.VMEM((chunks, tokens, blocks * rows), jnp.bfloat16),
            pltpu.SemaphoreType.DMA((chunks,)),
            pltpu.VMEM((out_rows, out_cols), jnp.float32),
        ],
        compiler_params=params(),
        cost_estimate=pl.CostEstimate(
            flops=2 * out_rows * out_cols * width,
            bytes_accessed=2 * width * (out_rows + cols),
            transcendentals=0,
        ),
        name="project",
    )(info, *left, bias.reshape(1, -1), *[own[k] for k in keys], *[copied[k] for k in keys])


def attend_kernel(tokens, slots, beacons, first_row, info, ratios, queries, *rest):
    pair, beside, across, corner = rest[:4]
    beacon_refs, out = rest[4 : 4 + beacons], rest[4 + beacons]
    place = 2 * info[7] + info[6]
    big = info[4]
    scale = 1.0 / math.sqrt(HEAD_DIM)
    tile = min(256, tokens)

    def pieces(variant):
        full = []
        if variant in (1, 3):
            full.append(beside)
        if variant in (2, 3):
            full += [across, corner]
        return full

    def score(rows, keys):
        return lax.dot_general(
            rows, keys, (((1,), (1,)), ((), ())), preferred_element_type=jnp.float32
        ) * scale

    def run(variant):
        for local_start in range(0, out.shape[0], tile):
            start = first_row + local_start
            rows = queries[start : start + tile, :]
            parts = []
            seen = start + tile
            scores = score(rows, pair[:seen, :HEAD_DIM])
            q_pos = start + lax.broadcasted_iota(jnp.int32, (tile, seen), 0)
            k_pos = lax.broadcasted_iota(jnp.int32, (tile, seen), 1)
            parts.append((jnp.where(k_pos <= q_pos, scores, -1e30), pair[:seen, HEAD_DIM:]))
            for ref in pieces(variant):
                parts.append((score(rows, ref[:tokens, :HEAD_DIM]), ref[:tokens, HEAD_DIM:]))
            for m in range(beacons):
                source = big ^ (m + 1)
                count = beacon_refs[m].shape[0]
                live = jnp.where(source < big, tokens // ratios[source], 0)
                local = lax.broadcasted_iota(jnp.int32, (tile, count), 1) % slots
                scores = score(rows, beacon_refs[m][:, :HEAD_DIM])
                parts.append((jnp.where(local < live, scores, -1e30), beacon_refs[m][:, HEAD_DIM:]))
            top = functools.reduce(
                jnp.maximum, [jnp.max(s, axis=1, keepdims=True) for s, _ in parts]
            )
            total = jnp.zeros((tile, 1), jnp.float32)
            mixed = jnp.zeros((tile, HEAD_DIM), jnp.float32)
            for scores, values in parts:
                weights = jnp.exp(scores - top)
                total += jnp.sum(weights, axis=1, keepdims=True)
                mixed += jnp.dot(
                    weights.astype(jnp.bfloat16), values, preferred_element_type=jnp.float32
                )
            out[local_start : local_start + tile, :] = (mixed / total).astype(jnp.bfloat16)

    for variant in range(SPLIT):
        pl.when(place == variant)(functools.partial(run, variant))


def attend(first_row, row_count, info, ratios, queries, keyvals, beacons):
    tokens, cols = queries.shape
    slots = keyvals[0].shape[0] - tokens
    heads = cols // HEAD_DIM
    keys = 4 * tokens + sum(b.shape[0] for b in beacons)
    return pl.pallas_call(
        functools.partial(attend_kernel, tokens, slots, len(beacons), first_row),
        grid=(heads,),
        out_shape=jax.ShapeDtypeStruct((row_count, cols), jnp.bfloat16),
        in_specs=[smem(), smem(), pl.BlockSpec((tokens, HEAD_DIM), lambda i: (0, i))]
        + [vmem()] * (len(keyvals) + len(beacons)),
        out_specs=pl.BlockSpec((row_count, HEAD_DIM), lambda i: (0, i)),
        compiler_params=params(),
        cost_estimate=pl.CostEstimate(
            flops=4 * row_count * keys * cols,
            bytes_accessed=4 * tokens * cols,
            transcendentals=row_count * keys * heads,
        ),
        name="attend",
    )(info, ratios, queries, *keyvals, *beacons)


def out_kernel(keys, info, attention, *rest):
    refs, (away, kept, weights, sems) = rest[:-4], rest[-4:]
    rows = refs[0].shape[0]
    width = kept.shape[2]
    per_group = width // rows

    for i, key in enumerate(keys):
        block = block_of(info, key)
        group = (block // per_group) ^ (2 * info[1] + info[7])
        spot = pl.multiple_of((block % per_group) * rows, 16)
        pltpu.make_async_copy(
            refs[i], weights.at[group, pl.ds(spot, rows), :], sems.at[group]
        ).start()
    for out, j, group in ((away, 1, 3), (away, 0, 1), (kept, 1, 2), (kept, 0, 0)):
        pltpu.make_async_copy(weights.at[group], weights.at[group], sems.at[group]).wait()
        out[j] = lax.dot_general(
            attention[...],
            weights[group],
            (((1,), (1,)), ((), ())),
            preferred_element_type=jnp.float32,
        ).astype(jnp.bfloat16)


def out_project(info, attention, pieces):
    tokens, depth = attention.shape
    keys = tuple(pieces)
    width = len(keys) * pieces[keys[0]].shape[0] // KVH
    shape = jax.ShapeDtypeStruct((2, tokens, width), jnp.bfloat16)
    return pl.pallas_call(
        functools.partial(out_kernel, keys),
        out_shape=(shape, shape),
        in_specs=[smem(), vmem()] + [hbm()] * len(keys),
        out_specs=(vmem(), vmem()),
        scratch_shapes=[
            pltpu.VMEM((KVH, width, depth), jnp.bfloat16),
            pltpu.SemaphoreType.DMA((KVH,)),
        ],
        compiler_params=params(),
        cost_estimate=pl.CostEstimate(
            flops=8 * tokens * width * depth, bytes_accessed=8 * width * depth, transcendentals=0
        ),
        name="out_project",
    )(info, attention, *[pieces[k] for k in keys])


def together(*values):
    return lax.optimization_barrier(values)


def on_device(
    hidden,
    norm_gain,
    query_weight,
    query_bias,
    keyval_weight,
    keyval_bias,
    beacon_weight,
    beacon_bias,
    out_weight,
    ratios,
):
    n_seq = lax.axis_size("seq")
    rows_dev = hidden.shape[0]
    half = rows_dev // 2
    seq_index = lax.axis_index("seq")
    head_index = lax.axis_index("head")
    big, l, x = seq_index // 4, (seq_index // 2) % 2, seq_index % 2
    y, c = head_index // 2, head_index % 2
    matched = c == l
    segment_ids = jnp.arange(ratios.shape[0], dtype=jnp.int32)
    own_ratio = jnp.sum(jnp.where(segment_ids == big, ratios, 0))
    inner = big != l
    info = jnp.stack(
        [
            matched.astype(jnp.int32),
            y,
            own_ratio,
            rows_dev // own_ratio,
            big,
            l,
            x,
            c,
        ]
    ).astype(jnp.int32)

    kv_cols = 2 * keyval_weight.shape[2]
    depth = keyval_weight.shape[0]
    query_cols = query_weight.shape[1]
    biases = jnp.concatenate([query_bias, keyval_bias.reshape(-1), beacon_bias.reshape(-1)])
    shard = jnp.concatenate(
        [
            query_weight,
            keyval_weight.reshape(depth, kv_cols),
            beacon_weight.reshape(depth, kv_cols),
        ],
        axis=1,
    )
    out_shard = out_weight.T

    def to_other_l(value):
        return send(value, n_seq, lambda big, l, x, y, c: (big, 1 - l, x, y, c) if c != l else None)

    def to_other_big(value, bit):
        return send(value, n_seq, lambda big, l, x, y, c: (big ^ bit, l, x, y, c) if c == l else None)

    def to_other_x(value):
        return send(value, n_seq, lambda big, l, x, y, c: (big, l, 1 - x, y, c) if c == l else None)

    def to_other_core(value):
        return send(value, n_seq, lambda big, l, x, y, c: (big, l, x, y, 1 - c) if c == l else None)

    def swap_l(value):
        return send(value, n_seq, lambda big, l, x, y, c: (big, 1 - l, x, y, c))

    def swap_big(value, bit):
        return send(value, n_seq, lambda big, l, x, y, c: (big ^ bit, l, x, y, c))

    def swap_inner(value):
        return send(
            value, n_seq, lambda big, l, x, y, c: (1 - big, 1 - l, x, y, c) if big != l else None
        )

    def to_outer(value):
        return send(value, n_seq, lambda big, l, x, y, c: (big, 1 - l, x, y, c) if big != l else None)

    def swap_x(value):
        return send(value, n_seq, lambda big, l, x, y, c: (big, l, 1 - x, y, c))

    own, copied = {(0, 0, 0): shard}, {}
    own_half = lax.dynamic_slice_in_dim(hidden, y * half, half, 0)
    first = send(
        own_half, n_seq, lambda big, l, x, y, c: (big, 1 - l, x, y, 1 - c) if c != l else None
    )
    own[0, 1, 0] = to_other_l(shard)
    own[1, 0, 0] = to_other_big(shard, 1)
    own[0, 0, 1] = to_other_x(shard)
    half_rows = out_shard.shape[0] // 2
    upper = swap_x(out_shard[:half_rows])
    gain = norm_gain.reshape(1, -1)
    own[0, 1, 0], own[1, 0, 0], own[0, 0, 1], upper, out_shard, gain, info = together(
        own[0, 1, 0], own[1, 0, 0], own[0, 0, 1], upper, out_shard, gain, info
    )
    lower = swap_x(out_shard[half_rows:])
    other_biases = send(biases, n_seq, lambda big, l, x, y, c: (big, l, x, y, 1 - c))
    biases = jnp.where(matched, biases, other_biases)
    own[1, 1, 0] = to_other_big(own[0, 1, 0], 1)
    own[0, 1, 1] = to_other_x(own[0, 1, 0])
    own[1, 0, 1] = to_other_x(own[1, 0, 0])
    keys = ((0, 0, 0), (0, 1, 0), (1, 0, 0), (0, 0, 1))
    for key in keys:
        copied[key] = to_other_core(own[key])
    (
        own[1, 1, 0],
        own[0, 1, 1],
        own[1, 0, 1],
        first,
        biases,
        lower,
        copied[0, 0, 0],
        copied[0, 1, 0],
        copied[1, 0, 0],
        copied[0, 0, 1],
    ) = together(
        own[1, 1, 0],
        own[0, 1, 1],
        own[1, 0, 1],
        first,
        biases,
        lower,
        *[copied[key] for key in keys],
    )
    own[1, 1, 1] = to_other_x(own[1, 1, 0])
    second = send(first, n_seq, lambda big, l, x, y, c: (big, l, x, 1 - y, c) if c != l else None)
    keys = ((1, 1, 0), (0, 1, 1), (1, 0, 1))
    for key in keys:
        copied[key] = to_other_core(own[key])
    copied[1, 1, 0], copied[0, 1, 1], copied[1, 0, 1], out_shard = together(
        *[copied[key] for key in keys], out_shard
    )
    outs = {(0, 0, 0): out_shard, (0, 1, 0): swap_l(out_shard)}
    two_segments = n_seq == 2 * SPLIT
    middle_own = swap_inner(out_shard) if two_segments else out_shard
    outs[0, 0, 1] = jnp.concatenate([upper, lower], axis=0)
    bit = 2
    while bit < n_seq // SPLIT:
        for key in list(own):
            new = (key[0] ^ bit, key[1], key[2])
            own[new] = to_other_big(own[key], bit)
            copied[new] = to_other_core(own[new])
        bit *= 2

    normed, pooled = norm_and_pool(info, hidden, first, second, gain)
    if two_segments:
        normed, middle_own, outs[0, 1, 0], own[1, 1, 1] = together(
            normed, middle_own, outs[0, 1, 0], own[1, 1, 1]
        )
        middle_other = swap_inner(outs[0, 1, 0])
        outer_own = to_outer(middle_own)
        outs[0, 1, 1] = swap_x(outs[0, 1, 0])
    copied[1, 1, 1] = to_other_core(own[1, 1, 1])
    slots_dev = rows_dev // R_MIN
    copied = {key: copied[key] for key in own}
    keyval = project(
        functools.partial(keyval_kernel, query_cols),
        rows_dev + slots_dev,
        kv_cols,
        info,
        [normed, pooled],
        biases[query_cols:],
        own,
        copied,
    )
    beside = send(keyval, n_seq, lambda big, l, x, y, c: (big, l, 1 - x, y, c))
    across = send(keyval, n_seq, lambda big, l, x, y, c: (big, l, x, y, 1 - c))
    normed, keyval = together(normed, keyval)
    query = project(
        functools.partial(query_kernel, 0),
        rows_dev,
        query_cols,
        info,
        [normed],
        biases[:query_cols],
        own,
        copied,
    )
    query, beside, across = together(query, beside, across)
    corner = send(beside, n_seq, lambda big, l, x, y, c: (big, l, x, y, 1 - c))
    beacons = [
        jnp.concatenate([piece[rows_dev:] for piece in (keyval, beside, across, corner)], axis=0)
    ]
    bit = 1
    while bit < n_seq // SPLIT:
        beacons += [swap_big(piece, bit) for piece in beacons]
        bit *= 2
    beacons = beacons[1:]
    if two_segments:
        query, middle_other, outer_own, outs[0, 1, 1] = together(
            query, middle_other, outer_own, outs[0, 1, 1]
        )
        outer_other = to_outer(middle_other)
        outs[1, 0, 0] = jnp.where(inner, middle_other, outer_own)
        outs[1, 0, 1] = swap_x(outs[1, 0, 0])
    else:
        bit = 1
        while bit < n_seq // SPLIT:
            for key in list(outs):
                if key[2] == 0:
                    outs[key[0] ^ bit, key[1], 0] = swap_big(outs[key], bit)
            bit *= 2
        for key in list(outs):
            if (key[0], key[1], 1) not in outs:
                outs[key[0], key[1], 1] = swap_x(outs[key])

    def attend_rows(first_row, row_count):
        return attend(
            first_row, row_count, info, ratios, query, [keyval, beside, across, corner], beacons
        )

    def swap_back(value):
        return send(
            value, n_seq, lambda big, l, x, y, c: (big, 1 - l, x, y, 1 - c) if c != l else None
        )

    def swap_core(value):
        return send(value, n_seq, lambda big, l, x, y, c: (big, l, x, y, 1 - c))

    def swap_y(value):
        return send(value, n_seq, lambda big, l, x, y, c: (big, l, x, 1 - y, c))

    def add(kept, from_core):
        sums = kept.astype(jnp.float32) + from_core.astype(jnp.float32)
        return sums[0], sums[1].astype(jnp.bfloat16)

    part = rows_dev // 2
    early = attend_rows(0, part)
    if two_segments:
        early, outer_other, outs[1, 0, 1] = together(early, outer_other, outs[1, 0, 1])
        outs[1, 1, 0] = jnp.where(inner, middle_own, outer_other)
        outs[1, 1, 1] = swap_x(outs[1, 1, 0])
    early_swapped = swap_back(early)
    query, early = together(query, early)
    late = attend_rows(part, part)
    late, early, early_swapped = together(late, early, early_swapped)
    late_swapped = swap_back(late)
    early_away, early_kept = out_project(info, jnp.where(matched, early, early_swapped), outs)
    early_away, early_kept, late, late_swapped = together(
        early_away, early_kept, late, late_swapped
    )
    early_near, early_far = add(early_kept, swap_core(early_away))
    late = jnp.where(matched, late, late_swapped)
    late, early_near, early_far = together(late, early_near, early_far)
    early_from_y = swap_y(early_far)
    late_away, late_kept = out_project(info, late, outs)
    late_away, late_kept, early_from_y = together(late_away, late_kept, early_from_y)
    late_near, late_far = add(late_kept, swap_core(late_away))
    results = [(early_near, early_from_y), (late_near, swap_y(late_far))]
    return jnp.concatenate(
        [(near + from_y.astype(jnp.float32)).astype(jnp.bfloat16) for near, from_y in results], axis=0
    )


def solution(mesh):
    return jax.shard_map(
        on_device,
        mesh=mesh,
        in_specs=(
            P("seq", None),
            P(),
            P("seq", "head"),
            P("head"),
            P("seq", None, "head"),
            P(None, "head"),
            P("seq", None, "head"),
            P(None, "head"),
            P("head", "seq"),
            P(),
        ),
        out_specs=P("seq", "head"),
        check_vma=False,
    )
```

```python
import functools
import math

import jax
import jax.numpy as jnp
from jax import lax
from jax.experimental import pallas as pl
from jax.experimental.pallas import tpu as pltpu
from jax.sharding import PartitionSpec as P

QH = 28
KVH = 4
HEAD_DIM = 128
SPLIT = 4
R_MIN = 8
AXES = ("seq", "head")
VMEM_LIMIT = 56 * 1024 * 1024


def params():
    return pltpu.CompilerParams(vmem_limit_bytes=VMEM_LIMIT)


def vmem():
    return pl.BlockSpec(memory_space=pltpu.VMEM)


def smem():
    return pl.BlockSpec(memory_space=pltpu.SMEM)


def hbm():
    return pl.BlockSpec(memory_space=pl.ANY)


def moves(n_seq, rule):
    pairs = []
    for s in range(n_seq):
        for h in range(KVH):
            target = rule(s >> 2, (s >> 1) & 1, s & 1, h >> 1, h & 1)
            if target is not None:
                big, l, x, y, c = target
                pairs.append((s * KVH + h, (4 * big + 2 * l + x) * KVH + 2 * y + c))
    return pairs


def send(value, n_seq, rule):
    return lax.ppermute(value, AXES, moves(n_seq, rule))


def norm_kernel(info, hidden, first, second, gain, normed, pooled, buf, sems):
    rows = hidden.shape[0]
    half = rows // 2
    tiles = sems.shape[0]
    tile = rows // tiles
    matched, y_bit, ratio = info[0], info[1], info[2]

    def land(i):
        return buf.at[pl.ds(i * tile, tile), :]

    for i in range(tiles):

        @pl.when(matched == 1)
        def _():
            pltpu.make_async_copy(hidden.at[pl.ds(i * tile, tile), :], land(i), sems.at[i]).start()

        upper = (i * tile) // half
        local = pl.ds(i * tile - upper * half, tile)

        @pl.when((matched == 0) & (y_bit == upper))
        def _():
            pltpu.make_async_copy(first.at[local, :], land(i), sems.at[i]).start()

        @pl.when((matched == 0) & (y_bit != upper))
        def _():
            pltpu.make_async_copy(second.at[local, :], land(i), sems.at[i]).start()

    scale = gain[...]
    for i in range(tiles):
        pltpu.make_async_copy(hidden.at[pl.ds(i * tile, tile), :], land(i), sems.at[i]).wait()
        floats = buf[i * tile : (i + 1) * tile, :].astype(jnp.float32)
        mean = jnp.mean(floats * floats, axis=1, keepdims=True)
        normed[i * tile : (i + 1) * tile, :] = (floats * lax.rsqrt(mean + 1e-06) * scale).astype(
            jnp.bfloat16
        )
    slots = pooled.shape[0]
    token = lax.broadcasted_iota(jnp.int32, (slots, rows), 1)
    slot = lax.broadcasted_iota(jnp.int32, (slots, rows), 0)
    member = (
        (token >= slot * ratio) & (token < (slot + 1) * ratio) & (slot < info[3])
    ).astype(jnp.float32).astype(jnp.bfloat16)
    total = jnp.dot(member, normed[...], preferred_element_type=jnp.float32)
    pooled[...] = (total / ratio.astype(jnp.float32)).astype(jnp.bfloat16)


def norm_and_pool(info, hidden, first, second, gain):
    rows, width = hidden.shape
    tiles = 8
    return pl.pallas_call(
        norm_kernel,
        out_shape=(
            jax.ShapeDtypeStruct((rows, width), jnp.bfloat16),
            jax.ShapeDtypeStruct((rows // R_MIN, width), jnp.bfloat16),
        ),
        in_specs=[smem(), hbm(), hbm(), hbm(), vmem()],
        out_specs=(vmem(), vmem()),
        scratch_shapes=[pltpu.VMEM((rows, width), jnp.bfloat16), pltpu.SemaphoreType.DMA((tiles,))],
        compiler_params=params(),
        cost_estimate=pl.CostEstimate(
            flops=2 * rows * rows // R_MIN * width, bytes_accessed=4 * rows * width, transcendentals=0
        ),
        name="norm_pool",
    )(info, hidden, first, second, gain)


def block_of(info, key):
    return 4 * (info[4] ^ key[0]) + 2 * (info[5] ^ key[1]) + (info[6] ^ key[2])


def chunk_blocks(rows):
    blocks = 2
    while blocks * rows % 128:
        blocks *= 2
    return blocks


def load_chunks(info, keys, refs, weights, sems, normed, left, left_sems, first_col):
    count = len(keys)
    rows, cols = refs[0].shape[0], weights.shape[2]
    blocks = chunk_blocks(rows)
    chunks = count // blocks
    flips = [4 * key[0] + 2 * key[1] + key[2] for key in keys]

    def chunk_of(k):
        return block_of(info, (0, 0, 0)) // blocks ^ k

    def members(k):
        return [i for i in range(count) if flips[i] // blocks == k]

    def piece(ref, i, k):
        spot = block_of(info, keys[i]) % blocks * rows
        return pltpu.make_async_copy(
            ref.at[:, pl.ds(first_col, cols)],
            weights.at[k, pl.ds(pl.multiple_of(spot, 16), rows), :],
            sems.at[i],
        )

    def columns(k):
        start = pl.multiple_of(chunk_of(k) * (blocks * rows), 128)
        return pltpu.make_async_copy(
            normed.at[:, pl.ds(start, blocks * rows)], left.at[k], left_sems.at[k]
        )

    for k in range(chunks):
        columns(k).start()
        for i in members(k):
            pl.when(info[0] == 1)(piece(refs[i], i, k).start)
            pl.when(info[0] == 0)(piece(refs[count + i], i, k).start)

    def wait(k):
        columns(k).wait()
        for i in members(k):
            piece(refs[i], i, k).wait()

    return chunks, wait, chunk_of


def query_kernel(first_col, keys, info, normed, bias, *rest):
    refs, (out, weights, sems, left, left_sems, total) = rest[:-6], rest[-6:]
    chunks, wait, _ = load_chunks(
        info, keys, refs, weights, sems, normed, left, left_sems, first_col
    )
    for k in range(chunks):
        wait(k)
        product = jnp.dot(left[k], weights[k], preferred_element_type=jnp.float32)
        if k == 0:
            total[...] = product + bias[...]
        elif k < chunks - 1:
            total[...] += product
        else:
            out[...] = (total[...] + product).astype(jnp.bfloat16)


def keyval_kernel(first_col, keys, info, normed, pooled, bias, *rest):
    refs, (out, weights, sems, left, left_sems, total) = rest[:-6], rest[-6:]
    chunks, wait, chunk_of = load_chunks(
        info, keys, refs, weights, sems, normed, left, left_sems, first_col
    )
    tokens, depth = normed.shape[0], weights.shape[1]
    cols = out.shape[1]
    for k in range(chunks):
        wait(k)
        slots = pooled[:, pl.ds(pl.multiple_of(chunk_of(k) * depth, 128), depth)]
        product = jnp.dot(left[k], weights[k, :, :cols], preferred_element_type=jnp.float32)
        beacon = jnp.dot(slots, weights[k, :, cols:], preferred_element_type=jnp.float32)
        if k == 0:
            total[:tokens, :] = product + bias[:, :cols]
            total[tokens:, :] = beacon + bias[:, cols:]
        elif k < chunks - 1:
            total[:tokens, :] += product
            total[tokens:, :] += beacon
        else:
            out[:tokens, :] = (total[:tokens, :] + product).astype(jnp.bfloat16)
            out[tokens:, :] = (total[tokens:, :] + beacon).astype(jnp.bfloat16)


def project(kernel, out_rows, out_cols, info, left, bias, own, copied):
    keys = tuple(own)
    rows = own[keys[0]].shape[0]
    blocks = chunk_blocks(rows)
    tokens, width = left[0].shape
    cols = bias.shape[0]
    chunks = len(keys) // blocks
    return pl.pallas_call(
        functools.partial(kernel, keys),
        out_shape=jax.ShapeDtypeStruct((out_rows, out_cols), jnp.bfloat16),
        in_specs=[smem(), hbm()] + [vmem()] * len(left) + [hbm()] * (2 * len(keys)),
        out_specs=vmem(),
        scratch_shapes=[
            pltpu.VMEM((chunks, blocks * rows, cols), jnp.bfloat16),
            pltpu.SemaphoreType.DMA((len(keys),)),
            pltpu.VMEM((chunks, tokens, blocks * rows), jnp.bfloat16),
            pltpu.SemaphoreType.DMA((chunks,)),
            pltpu.VMEM((out_rows, out_cols), jnp.float32),
        ],
        compiler_params=params(),
        cost_estimate=pl.CostEstimate(
            flops=2 * out_rows * out_cols * width,
            bytes_accessed=2 * width * (out_rows + cols),
            transcendentals=0,
        ),
        name="project",
    )(info, *left, bias.reshape(1, -1), *[own[k] for k in keys], *[copied[k] for k in keys])


def attend_kernel(tokens, slots, beacons, first_row, info, ratios, queries, *rest):
    pair, beside, across, corner = rest[:4]
    beacon_refs, out = rest[4 : 4 + beacons], rest[4 + beacons]
    place = 2 * info[7] + info[6]
    big = info[4]
    scale = 1.0 / math.sqrt(HEAD_DIM)
    tile = min(256, tokens)

    def pieces(variant):
        full = []
        if variant in (1, 3):
            full.append(beside)
        if variant in (2, 3):
            full += [across, corner]
        return full

    def score(rows, keys):
        return lax.dot_general(
            rows, keys, (((1,), (1,)), ((), ())), preferred_element_type=jnp.float32
        ) * scale

    def run(variant):
        for local_start in range(0, out.shape[0], tile):
            start = first_row + local_start
            rows = queries[start : start + tile, :]
            parts = []
            seen = start + tile
            scores = score(rows, pair[:seen, :HEAD_DIM])
            q_pos = start + lax.broadcasted_iota(jnp.int32, (tile, seen), 0)
            k_pos = lax.broadcasted_iota(jnp.int32, (tile, seen), 1)
            parts.append((jnp.where(k_pos <= q_pos, scores, -1e30), pair[:seen, HEAD_DIM:]))
            for ref in pieces(variant):
                parts.append((score(rows, ref[:tokens, :HEAD_DIM]), ref[:tokens, HEAD_DIM:]))
            for m in range(beacons):
                source = big ^ (m + 1)
                count = beacon_refs[m].shape[0]
                live = jnp.where(source < big, tokens // ratios[source], 0)
                local = lax.broadcasted_iota(jnp.int32, (tile, count), 1) % slots
                scores = score(rows, beacon_refs[m][:, :HEAD_DIM])
                parts.append((jnp.where(local < live, scores, -1e30), beacon_refs[m][:, HEAD_DIM:]))
            top = functools.reduce(
                jnp.maximum, [jnp.max(s, axis=1, keepdims=True) for s, _ in parts]
            )
            total = jnp.zeros((tile, 1), jnp.float32)
            mixed = jnp.zeros((tile, HEAD_DIM), jnp.float32)
            for scores, values in parts:
                weights = jnp.exp(scores - top)
                total += jnp.sum(weights, axis=1, keepdims=True)
                mixed += jnp.dot(
                    weights.astype(jnp.bfloat16), values, preferred_element_type=jnp.float32
                )
            out[local_start : local_start + tile, :] = (mixed / total).astype(jnp.bfloat16)

    for variant in range(SPLIT):
        pl.when(place == variant)(functools.partial(run, variant))


def attend(first_row, row_count, info, ratios, queries, keyvals, beacons):
    tokens, cols = queries.shape
    slots = keyvals[0].shape[0] - tokens
    heads = cols // HEAD_DIM
    keys = 4 * tokens + sum(b.shape[0] for b in beacons)
    return pl.pallas_call(
        functools.partial(attend_kernel, tokens, slots, len(beacons), first_row),
        grid=(heads,),
        out_shape=jax.ShapeDtypeStruct((row_count, cols), jnp.bfloat16),
        in_specs=[smem(), smem(), pl.BlockSpec((tokens, HEAD_DIM), lambda i: (0, i))]
        + [vmem()] * (len(keyvals) + len(beacons)),
        out_specs=pl.BlockSpec((row_count, HEAD_DIM), lambda i: (0, i)),
        compiler_params=params(),
        cost_estimate=pl.CostEstimate(
            flops=4 * row_count * keys * cols,
            bytes_accessed=4 * tokens * cols,
            transcendentals=row_count * keys * heads,
        ),
        name="attend",
    )(info, ratios, queries, *keyvals, *beacons)


def out_kernel(y_flip, keys, info, attention, *rest):
    refs, (away, kept, weights, sems) = rest[:-4], rest[-4:]
    rows = refs[0].shape[0]
    width = kept.shape[1]
    per_group = width // rows

    for i, key in enumerate(keys):
        block = block_of(info, key)
        group = block // per_group
        side = (group % 2) ^ info[7]
        spot = pl.multiple_of((block % per_group) * rows, 16)
        copy = pltpu.make_async_copy(
            refs[i], weights.at[side, pl.ds(spot, rows), :], sems.at[side]
        )
        pl.when(group // 2 == (info[1] ^ y_flip))(copy.start)
    for out, side in ((away, 1), (kept, 0)):
        pltpu.make_async_copy(weights.at[side], weights.at[side], sems.at[side]).wait()
        out[...] = lax.dot_general(
            attention[...],
            weights[side],
            (((1,), (1,)), ((), ())),
            preferred_element_type=jnp.float32,
        ).astype(jnp.bfloat16)


def out_project(y_flip, info, attention, pieces):
    tokens, depth = attention.shape
    keys = tuple(pieces)
    width = len(keys) * pieces[keys[0]].shape[0] // KVH
    shape = jax.ShapeDtypeStruct((tokens, width), jnp.bfloat16)
    return pl.pallas_call(
        functools.partial(out_kernel, y_flip, keys),
        out_shape=(shape, shape),
        in_specs=[smem(), vmem()] + [hbm()] * len(keys),
        out_specs=(vmem(), vmem()),
        scratch_shapes=[
            pltpu.VMEM((2, width, depth), jnp.bfloat16),
            pltpu.SemaphoreType.DMA((2,)),
        ],
        compiler_params=params(),
        cost_estimate=pl.CostEstimate(
            flops=4 * tokens * width * depth, bytes_accessed=4 * width * depth, transcendentals=0
        ),
        name="out_project",
    )(info, attention, *[pieces[k] for k in keys])


def together(*values):
    return lax.optimization_barrier(values)


def on_device(
    hidden,
    norm_gain,
    query_weight,
    query_bias,
    keyval_weight,
    keyval_bias,
    beacon_weight,
    beacon_bias,
    out_weight,
    ratios,
):
    n_seq = lax.axis_size("seq")
    rows_dev = hidden.shape[0]
    half = rows_dev // 2
    seq_index = lax.axis_index("seq")
    head_index = lax.axis_index("head")
    big, l, x = seq_index // 4, (seq_index // 2) % 2, seq_index % 2
    y, c = head_index // 2, head_index % 2
    matched = c == l
    segment_ids = jnp.arange(ratios.shape[0], dtype=jnp.int32)
    own_ratio = jnp.sum(jnp.where(segment_ids == big, ratios, 0))
    inner = big != l
    info = jnp.stack(
        [
            matched.astype(jnp.int32),
            y,
            own_ratio,
            rows_dev // own_ratio,
            big,
            l,
            x,
            c,
        ]
    ).astype(jnp.int32)

    kv_cols = 2 * keyval_weight.shape[2]
    depth = keyval_weight.shape[0]
    query_cols = query_weight.shape[1]
    biases = jnp.concatenate([query_bias, keyval_bias.reshape(-1), beacon_bias.reshape(-1)])
    shard = jnp.concatenate(
        [
            query_weight,
            keyval_weight.reshape(depth, kv_cols),
            beacon_weight.reshape(depth, kv_cols),
        ],
        axis=1,
    )
    out_shard = out_weight.T

    def to_other_l(value):
        return send(value, n_seq, lambda big, l, x, y, c: (big, 1 - l, x, y, c) if c != l else None)

    def to_other_big(value, bit):
        return send(value, n_seq, lambda big, l, x, y, c: (big ^ bit, l, x, y, c) if c == l else None)

    def to_other_x(value):
        return send(value, n_seq, lambda big, l, x, y, c: (big, l, 1 - x, y, c) if c == l else None)

    def to_other_core(value):
        return send(value, n_seq, lambda big, l, x, y, c: (big, l, x, y, 1 - c) if c == l else None)

    def swap_l(value):
        return send(value, n_seq, lambda big, l, x, y, c: (big, 1 - l, x, y, c))

    def swap_big(value, bit):
        return send(value, n_seq, lambda big, l, x, y, c: (big ^ bit, l, x, y, c))

    def swap_inner(value):
        return send(
            value, n_seq, lambda big, l, x, y, c: (1 - big, 1 - l, x, y, c) if big != l else None
        )

    def to_outer(value):
        return send(value, n_seq, lambda big, l, x, y, c: (big, 1 - l, x, y, c) if big != l else None)

    def swap_x(value):
        return send(value, n_seq, lambda big, l, x, y, c: (big, l, 1 - x, y, c))

    own, copied = {(0, 0, 0): shard}, {}
    own_half = lax.dynamic_slice_in_dim(hidden, y * half, half, 0)
    first = send(
        own_half, n_seq, lambda big, l, x, y, c: (big, 1 - l, x, y, 1 - c) if c != l else None
    )
    own[0, 1, 0] = to_other_l(shard)
    own[1, 0, 0] = to_other_big(shard, 1)
    own[0, 0, 1] = to_other_x(shard)
    half_rows = out_shard.shape[0] // 2
    upper = swap_x(out_shard[:half_rows])
    gain = norm_gain.reshape(1, -1)
    own[0, 1, 0], own[1, 0, 0], own[0, 0, 1], upper, out_shard, gain, info = together(
        own[0, 1, 0], own[1, 0, 0], own[0, 0, 1], upper, out_shard, gain, info
    )
    lower = swap_x(out_shard[half_rows:])
    other_biases = send(biases, n_seq, lambda big, l, x, y, c: (big, l, x, y, 1 - c))
    biases = jnp.where(matched, biases, other_biases)
    own[1, 1, 0] = to_other_big(own[0, 1, 0], 1)
    own[0, 1, 1] = to_other_x(own[0, 1, 0])
    own[1, 0, 1] = to_other_x(own[1, 0, 0])
    keys = ((0, 0, 0), (0, 1, 0), (1, 0, 0), (0, 0, 1))
    for key in keys:
        copied[key] = to_other_core(own[key])
    (
        own[1, 1, 0],
        own[0, 1, 1],
        own[1, 0, 1],
        first,
        biases,
        lower,
        copied[0, 0, 0],
        copied[0, 1, 0],
        copied[1, 0, 0],
        copied[0, 0, 1],
    ) = together(
        own[1, 1, 0],
        own[0, 1, 1],
        own[1, 0, 1],
        first,
        biases,
        lower,
        *[copied[key] for key in keys],
    )
    own[1, 1, 1] = to_other_x(own[1, 1, 0])
    second = send(first, n_seq, lambda big, l, x, y, c: (big, l, x, 1 - y, c) if c != l else None)
    keys = ((1, 1, 0), (0, 1, 1), (1, 0, 1))
    for key in keys:
        copied[key] = to_other_core(own[key])
    copied[1, 1, 0], copied[0, 1, 1], copied[1, 0, 1], out_shard = together(
        *[copied[key] for key in keys], out_shard
    )
    outs = {(0, 0, 0): out_shard, (0, 1, 0): swap_l(out_shard)}
    two_segments = n_seq == 2 * SPLIT
    middle_own = swap_inner(out_shard) if two_segments else out_shard
    outs[0, 0, 1] = jnp.concatenate([upper, lower], axis=0)
    bit = 2
    while bit < n_seq // SPLIT:
        for key in list(own):
            new = (key[0] ^ bit, key[1], key[2])
            own[new] = to_other_big(own[key], bit)
            copied[new] = to_other_core(own[new])
        bit *= 2

    normed, pooled = norm_and_pool(info, hidden, first, second, gain)
    if two_segments:
        normed, middle_own, outs[0, 1, 0], own[1, 1, 1] = together(
            normed, middle_own, outs[0, 1, 0], own[1, 1, 1]
        )
        middle_other = swap_inner(outs[0, 1, 0])
        outer_own = to_outer(middle_own)
        outs[0, 1, 1] = swap_x(outs[0, 1, 0])
    copied[1, 1, 1] = to_other_core(own[1, 1, 1])
    slots_dev = rows_dev // R_MIN
    copied = {key: copied[key] for key in own}
    keyval = project(
        functools.partial(keyval_kernel, query_cols),
        rows_dev + slots_dev,
        kv_cols,
        info,
        [normed, pooled],
        biases[query_cols:],
        own,
        copied,
    )
    beside = send(keyval, n_seq, lambda big, l, x, y, c: (big, l, 1 - x, y, c))
    across = send(keyval, n_seq, lambda big, l, x, y, c: (big, l, x, y, 1 - c))
    normed, keyval = together(normed, keyval)
    query = project(
        functools.partial(query_kernel, 0),
        rows_dev,
        query_cols,
        info,
        [normed],
        biases[:query_cols],
        own,
        copied,
    )
    query, beside, across = together(query, beside, across)
    corner = send(beside, n_seq, lambda big, l, x, y, c: (big, l, x, y, 1 - c))
    beacons = [
        jnp.concatenate([piece[rows_dev:] for piece in (keyval, beside, across, corner)], axis=0)
    ]
    bit = 1
    while bit < n_seq // SPLIT:
        beacons += [swap_big(piece, bit) for piece in beacons]
        bit *= 2
    beacons = beacons[1:]
    if two_segments:
        query, middle_other, outer_own, outs[0, 1, 1] = together(
            query, middle_other, outer_own, outs[0, 1, 1]
        )
        outer_other = to_outer(middle_other)
        outs[1, 0, 0] = jnp.where(inner, middle_other, outer_own)
        outs[1, 0, 1] = swap_x(outs[1, 0, 0])
    else:
        bit = 1
        while bit < n_seq // SPLIT:
            for key in list(outs):
                if key[2] == 0:
                    outs[key[0] ^ bit, key[1], 0] = swap_big(outs[key], bit)
            bit *= 2
        for key in list(outs):
            if (key[0], key[1], 1) not in outs:
                outs[key[0], key[1], 1] = swap_x(outs[key])

    def attend_rows(first_row, row_count):
        return attend(
            first_row, row_count, info, ratios, query, [keyval, beside, across, corner], beacons
        )

    def swap_back(value):
        return send(
            value, n_seq, lambda big, l, x, y, c: (big, 1 - l, x, y, 1 - c) if c != l else None
        )

    def swap_core(value):
        return send(value, n_seq, lambda big, l, x, y, c: (big, l, x, y, 1 - c))

    def swap_y(value):
        return send(value, n_seq, lambda big, l, x, y, c: (big, l, x, 1 - y, c))

    def add(kept, from_core):
        return kept.astype(jnp.float32) + from_core.astype(jnp.float32)

    part = rows_dev // 2
    early = attend_rows(0, part)
    if two_segments:
        early, outer_other, outs[1, 0, 1] = together(early, outer_other, outs[1, 0, 1])
        outs[1, 1, 0] = jnp.where(inner, middle_own, outer_other)
        outs[1, 1, 1] = swap_x(outs[1, 1, 0])
    early_swapped = swap_back(early)
    query, early = together(query, early)
    late = attend_rows(part, part)
    late, early, early_swapped = together(late, early, early_swapped)
    late_swapped = swap_back(late)
    early = jnp.where(matched, early, early_swapped)
    early_away, early_kept = out_project(1, info, early, outs)
    early_away, early_kept, late_swapped = together(early_away, early_kept, late_swapped)
    late = jnp.where(matched, late, late_swapped)
    early_core = swap_core(early_away)
    late_away, late_kept = out_project(1, info, late, outs)
    late_away, late_kept, early_core = together(late_away, late_kept, early_core)
    early_far = add(early_kept, early_core).astype(jnp.bfloat16)
    early_from_y = swap_y(early_far)
    late_core = swap_core(late_away)
    late_core, early_far = together(late_core, early_far)
    late_far = add(late_kept, late_core).astype(jnp.bfloat16)
    early, late, late_far = together(early, late, late_far)
    late_from_y = swap_y(late_far)
    away, kept = out_project(0, info, jnp.concatenate([early, late], axis=0), outs)
    kept, away, early_from_y, late_from_y = together(kept, away, early_from_y, late_from_y)
    from_y = jnp.concatenate([early_from_y, late_from_y], axis=0)
    return (add(kept, swap_core(away)) + from_y.astype(jnp.float32)).astype(jnp.bfloat16)


def solution(mesh):
    return jax.shard_map(
        on_device,
        mesh=mesh,
        in_specs=(
            P("seq", None),
            P(),
            P("seq", "head"),
            P("head"),
            P("seq", None, "head"),
            P(None, "head"),
            P("seq", None, "head"),
            P(None, "head"),
            P("head", "seq"),
            P(),
        ),
        out_specs=P("seq", "head"),
        check_vma=False,
    )
```
